512 devices in a mesh: expert: 64 (over y, x, z_hi, core), mp: 8 (over z_lo).
Axes of the slice: x: 4, y: 4, z: 16 (z_hi: 2, z_lo: 8; z = z_hi * 8 + z_lo), core: 2. Of those that a mesh axis runs over, the one named last changes fastest.
Arguments:
- tokens: bfloat16 [8192, 3584], P('expert'), may hold values from -6 to 6
- routes: int32 [8192, 2], P('expert'), may hold values from 0 to 31, all different within a row; in each aligned block of 128 rows (0 to 127, 128 to 255, ...) at most 16 rows name the same one
- gate_values: float32 [8192, 2], P('expert'), may hold values from 0.2 to 1
- expert_weights: bfloat16 [64, 3, 1792, 1024], P('expert', None, None, 'mp'), may hold values from -0.09375 to 0.09375
- old_owner: int32 [32], replicated, may hold values from 0 to 31, as said below
- new_owner: int32 [32], replicated, may hold values from 0 to 31, as said below
Outputs:
- mixed: bfloat16 [8192, 3584], P('expert', 'mp')
- relocated: bfloat16 [64, 3, 1792, 1024], P('expert', None, None, 'mp')
The draws below stay inside these ranges and needn't reach their ends.
Inputs may be any that keep to these rules, and one draw needn't show every extreme that they name: `routes`: in each aligned block of 128 rows (the rows of one index of expert) no expert is named by more than 16 rows. `old_owner`: each slot holds exactly one expert. Each slot holds exactly one expert; exactly 2 experts have a new_owner other than their old_owner.
All inputs are finite; a program needn't handle non-finite values.
Results may differ from the reference program's by a relative error of at most 0.019.
Values may be sent and summed in bfloat16 or wider, within the bound.
No kernel may reach another device: no remote copies, remote signals or barrier semaphores. Data moves between devices by JAX's collectives and lax.ppermute only.
A program may use at most 64 MiB of HBM per device.

```python
import math
import jax
import jax.numpy as jnp
import numpy as np
from jax import lax

D = 3584
FF = 1024
TOP = 2
MOVES = 2
TOK_DEV = 128
EXPERTS = 32
TOKENS = 8192
CAP = 16
N_EXPERT = 64
N_MP = 8


def plan_pair(key):
    starting = jax.random.permutation(jax.random.fold_in(key, 11), EXPERTS).astype(jnp.int32)
    chosen = jax.random.permutation(jax.random.fold_in(key, 12), EXPERTS)[:MOVES]
    rotated = jnp.roll(chosen, 1)
    shifted = starting.at[chosen].set(starting[rotated])
    return (starting, shifted.astype(jnp.int32))


def draw_old_owner(key, part):
    return plan_pair(key)[0]


def draw_new_owner(key, part):
    return plan_pair(key)[1]


def level_of(rng, dims, cuts, smallest, largest):
    level = 1.0
    for axis_at, parts in cuts:
        heights = jax.random.uniform(jax.random.fold_in(jax.random.fold_in(rng, 6), axis_at), (parts,), jnp.float32, smallest / len(cuts), largest / len(cuts))
        level = level * jnp.repeat(jnp.exp(heights), dims[axis_at] // parts).reshape((-1,) + (1,) * (len(dims) - 1 - axis_at))
    return level


def assign_block(own_key, own, number, rows, amount, top, bound, slope):
    sequence = jax.random.permutation(own_key, amount)
    crowded, usual = shares(amount, rows * top, bound, slope, True), shares(amount, rows * top, bound, slope, False)
    places = jnp.arange(amount)

    def named(lengths, turn):
        used = int((lengths > 0).sum())
        fixed = max(1, used // 4)
        moved = fixed + (places - fixed + turn * (used - fixed)) % max(1, amount - fixed)
        return jnp.zeros((amount,), jnp.int32).at[sequence[jnp.where(places < fixed, places, moved)]].set(jnp.asarray(lengths, jnp.int32))

    lengths = jnp.where(number % 4 == 0, named(crowded, number // 4), named(usual, number - number // 4 - 1))
    mixed = jax.random.permutation(jax.random.fold_in(own, 3), amount)
    giver, taker = mixed[0:amount // 2 * 2:2], mixed[1:amount // 2 * 2:2]
    room = jnp.minimum(lengths[giver] - 1, bound - lengths[taker]) // 2
    room = jnp.where((giver == sequence[0]) | (taker == sequence[0]) | (lengths[taker] == 0), 0, jnp.maximum(room, 0))
    moved = jax.random.randint(jax.random.fold_in(own, 4), (amount // 2,), 0, 1 << 20) % (room + 1)
    lengths = lengths.at[giver].add(-moved).at[taker].add(moved)
    items = jnp.searchsorted(jnp.cumsum(lengths), jnp.arange(rows * top), side="right").astype(jnp.int32)
    listing = items.reshape(top, rows).T
    listing = listing[jax.random.permutation(jax.random.fold_in(own, 1), rows)]
    turn = jax.random.randint(jax.random.fold_in(own, 2), (rows, 1), 0, top)
    return jnp.take_along_axis(listing, (jnp.arange(top)[None, :] + turn) % top, axis=1)


def shares(count, total, bound, skew, full):
    loads = [(1 << 20) // math.isqrt(grade ** skew) + 1 for grade in range(1, count + 1)]
    largest = bound if full else min(bound, max(-(-total // count), total * loads[0] // sum(loads)))
    least = 1 if total - largest >= count - 1 else 0
    holding, rest = [largest] + [least] * (count - 1), total - largest - least * (count - 1)
    while rest > 0:
        free = [i for i in range(1, count) if holding[i] < largest] or [i for i in range(1, count) if holding[i] < bound]
        whole, left = sum([loads[i] for i in free]), rest
        for i in free:
            addition = min(bound - holding[i], max(1, left * loads[i] // whole), rest)
            holding[i] = holding[i] + addition
            rest = rest - addition
    return np.array(holding)


def gaussian(key, extent, spread, most, split=(), kind=jnp.bfloat16):
    factor_of = level_of(key, extent, split, -0.22, 0.18) if split else 1.0
    entries = jax.random.normal(key, extent, jnp.float32) * spread * factor_of
    return jnp.minimum(jnp.maximum(entries, -most), most).astype(kind)


def setup_inputs(seed: int = 0) -> dict:
    splits = jax.random.split(jax.random.key(seed), 7)
    tokens = gaussian(splits[0], (TOKENS, D), 1.0, 6.0, ((0, 64),))
    routes_keys = jax.random.split(jax.random.fold_in(splits[1], 1), TOKENS // TOK_DEV)
    routes_turns = jax.random.permutation(jax.random.fold_in(splits[1], 3), TOKENS // TOK_DEV)
    routes = jax.vmap(lambda own, number: assign_block(jax.random.fold_in(splits[1], 2), own, number, TOK_DEV, EXPERTS, TOP, CAP, 2))(routes_keys, routes_turns).reshape((TOKENS, TOP))
    gate_values = jnp.clip(0.2 + 0.8 * jax.random.uniform(splits[2], (TOKENS, TOP), jnp.float32) ** level_of(splits[2], (TOKENS, TOP), ((0, 64),), -0.2, 0.2), 0.2, 1.0)
    expert_weights = gaussian(splits[3], (N_EXPERT, 3, D // 2, FF), D ** -0.5, 0.09375, ((0, 64), (3, 8)))
    old_owner = draw_old_owner(jax.random.fold_in(splits[6], 71), 0)
    new_owner = draw_new_owner(jax.random.fold_in(splits[6], 71), 0)
    return {"tokens": tokens, "routes": routes, "gate_values": gate_values, "expert_weights": expert_weights, "old_owner": old_owner, "new_owner": new_owner}


def one_expert(packed):
    row_block, weights = packed
    gate_sum = jnp.dot(row_block, weights[0], preferred_element_type=jnp.float32)
    up_sum = jnp.dot(row_block, weights[1], preferred_element_type=jnp.float32)
    hidden = (jax.nn.silu(gate_sum) * up_sum).astype(jnp.bfloat16)
    group_width = FF // N_MP
    running = jnp.zeros((row_block.shape[0], D), jnp.float32)
    for group_index in range(N_MP):
        low_unit = group_index * group_width
        partial_out = lax.dot_general(hidden[:, low_unit:low_unit + group_width], weights[2][:, low_unit:low_unit + group_width], (((1,), (1,)), ((), ())), preferred_element_type=jnp.float32)
        rounded = lax.optimization_barrier(partial_out.astype(jnp.bfloat16))
        running = running + rounded.astype(jnp.float32)
    return running.astype(jnp.bfloat16)


def reference(tokens, routes, gate_values, expert_weights, old_owner, new_owner):
    slot_ids = jnp.arange(EXPERTS, dtype=jnp.int32)
    newcomer = jnp.sum(jnp.where(new_owner[None, :] == slot_ids[:, None], slot_ids[None, :], 0), axis=1).astype(jnp.int32)
    source_slot = old_owner[newcomer]
    source_rows = (2 * source_slot[:, None] + jnp.arange(2, dtype=jnp.int32)[None, :]).reshape(-1).astype(jnp.int32)
    relocated = expert_weights[source_rows]
    sub_cols = D // (2 * N_MP)
    shaped = expert_weights.reshape(EXPERTS, 2, 3, N_MP, sub_cols, FF)
    assembled = jnp.transpose(shaped, (0, 2, 3, 1, 4, 5)).reshape(EXPERTS, 3, D, FF)
    by_expert = assembled[old_owner]
    per_device = routes.reshape(N_EXPERT, TOK_DEV * TOP)
    onehot = (per_device[:, :, None] == slot_ids[None, None, :]).astype(jnp.int32)
    rank_in = jnp.sum((jnp.cumsum(onehot, axis=1) - onehot) * onehot, axis=2)
    row_index = (jnp.arange(N_EXPERT, dtype=jnp.int32)[:, None] * CAP + rank_in).reshape(-1).astype(jnp.int32)
    expert_index = routes.reshape(-1).astype(jnp.int32)
    token_index = jnp.arange(TOKENS * TOP, dtype=jnp.int32) // TOP
    buffers = jnp.zeros((EXPERTS, N_EXPERT * CAP, D), tokens.dtype).at[expert_index, row_index].set(tokens[token_index])
    outputs = lax.map(one_expert, (buffers, by_expert))
    picked = outputs[expert_index, row_index].astype(jnp.float32)
    mixed = jnp.sum(picked.reshape(TOKENS, TOP, D) * gate_values[:, :, None].astype(jnp.float32), axis=1)
    return mixed.astype(jnp.bfloat16), relocated
```

```python
import jax
import jax.numpy as jnp
from jax import lax
from jax.sharding import Mesh, PartitionSpec as P

PLANE = ("y", "x", "c")
RING = ("zh", "mp")
CAP = 16


def swap(value, axis):
    return lax.ppermute(value, axis, [(0, 1), (1, 0)])


def place_codes(routes, gate_values, owner):
    experts = owner.shape[0]
    flat = routes.T.reshape(-1)
    count = flat.shape[0]
    ids = jnp.arange(experts, dtype=jnp.int32)
    hot = (flat[:, None] == ids[None, :]).astype(jnp.bfloat16)
    at = jnp.arange(count, dtype=jnp.int32)
    earlier = (at[:, None] > at[None, :]).astype(jnp.bfloat16)
    before = jnp.dot(earlier, hot, preferred_element_type=jnp.float32)
    code = jnp.sum(hot.astype(jnp.float32) * (before + (owner * CAP).astype(jnp.float32)[None, :]), axis=1)
    return jnp.concatenate([code.reshape(routes.shape[1], -1), gate_values.T], axis=0)


def placed_rows(codes, zh):
    code = codes[:2].astype(jnp.int32)
    slot, rank = code // CAP, code % CAP
    row = jnp.where(slot % 2 == zh, (slot // 2) * (2 * CAP) + rank, -2 * CAP)
    return jnp.stack([row, row + CAP], axis=1).reshape(2, -1)


def send_rows(rows, table):
    total = 2 * CAP * lax.axis_size("y") * lax.axis_size("x")
    at = jnp.arange(total, dtype=jnp.int32)
    pick = ((rows[0][None, :] == at[:, None]) | (rows[1][None, :] == at[:, None])).astype(jnp.bfloat16)
    out = jnp.dot(pick, table, preferred_element_type=jnp.float32).astype(jnp.bfloat16)
    out = out.reshape(total // CAP, CAP, -1)
    return lax.all_to_all(out, PLANE, split_axis=0, concat_axis=0, tiled=True).reshape(total, -1)


def expert_part(rows, weights):
    half = jnp.einsum("rd,gdf->grf", rows, weights[:2], preferred_element_type=jnp.float32)
    total = half + swap(half, "c")
    hidden = (jax.nn.silu(total[0]) * total[1]).astype(jnp.bfloat16)
    return lax.dot_general(
        hidden, weights[2], (((1,), (1,)), ((), ())), preferred_element_type=jnp.float32
    ).astype(jnp.bfloat16)


def return_rows(out, codes, rows):
    total = out.shape[0]
    back = lax.all_to_all(
        out.reshape(total // CAP, CAP, -1), PLANE, split_axis=0, concat_axis=0, tiled=True
    ).reshape(total, -1)
    at = jnp.arange(total, dtype=jnp.int32)
    gate = jnp.concatenate([codes[2:4], codes[2:4]], axis=1)
    mix = sum(jnp.where(rows[k][:, None] == at[None, :], gate[k][:, None], 0.0) for k in range(2))
    high = mix.astype(jnp.bfloat16)
    low = (mix - high.astype(jnp.float32)).astype(jnp.bfloat16)
    return jnp.dot(high, back, preferred_element_type=jnp.float32) + jnp.dot(
        low, back, preferred_element_type=jnp.float32
    )


def by_columns(mixed, groups):
    parts = mixed.astype(jnp.bfloat16).reshape(2, mixed.shape[0] // 2, groups, -1)
    return jnp.transpose(parts, (2, 1, 0, 3)).reshape(groups, mixed.shape[0] // 2, -1)


def relocate(own, old_owner, new_owner):
    chips = lax.axis_size("y") * lax.axis_size("x")
    zh = lax.axis_index("zh")
    moved = new_owner != old_owner
    low = jnp.min(jnp.where(moved, old_owner, old_owner.shape[0]))
    high = jnp.max(jnp.where(moved, old_owner, -1))
    pieces = own.reshape(chips, -1, own.shape[-1])
    spread = lax.all_to_all(pieces, ("y", "x"), split_axis=0, concat_axis=0, tiled=True)
    low_piece = lax.dynamic_index_in_dim(spread, low // 2, 0, keepdims=False)
    high_piece = lax.dynamic_index_in_dim(spread, high // 2, 0, keepdims=False)
    low_here, high_here = low % 2 == zh, high % 2 == zh
    other = swap(jnp.where(low_here, low_piece, high_piece), "zh")
    to_low = jnp.where(high_here, high_piece, other)
    to_high = jnp.where(low_here, low_piece, other)
    slots = 2 * jnp.arange(chips, dtype=jnp.int32)[:, None, None] + zh
    chosen = jnp.where(slots == low, to_low[None], jnp.where(slots == high, to_high[None], spread))
    arrived = lax.all_to_all(chosen, ("y", "x"), split_axis=0, concat_axis=0, tiled=True)
    return arrived.reshape(own.shape)


def shards(tokens, routes, gate_values, expert_weights, old_owner, new_owner):
    zh, lane = lax.axis_index("zh"), lax.axis_index("mp")
    groups = lax.axis_size("mp")
    tok_rows, width = tokens.shape
    own = expert_weights[0]
    codes = place_codes(routes, gate_values, old_owner)
    other_codes = swap(codes, "zh")
    table = jnp.transpose(tokens.reshape(tok_rows, groups, 2, -1), (2, 0, 1, 3)).reshape(2 * tok_rows, -1)
    share = 2 * tok_rows // groups
    ring = lax.all_gather(lax.dynamic_slice_in_dim(table, lane * share, share, 0), RING)
    rows = placed_rows(codes, zh)
    mixed = return_rows(expert_part(send_rows(rows, table), own), codes, rows)
    mixed = by_columns(mixed, groups)

    other_table = lax.dynamic_slice_in_dim(ring, (1 - zh) * groups, groups, 0).reshape(2 * tok_rows, -1)
    other_rows = placed_rows(other_codes, zh)
    other_mixed = return_rows(expert_part(send_rows(other_rows, other_table), own), other_codes, other_rows)
    other_mixed = by_columns(other_mixed, groups)
    both = jnp.concatenate(
        [jnp.where(zh == 0, mixed, other_mixed), jnp.where(zh == 0, other_mixed, mixed)], axis=0
    )
    both, own = lax.optimization_barrier((both, own))
    out = lax.psum_scatter(both, RING, scatter_dimension=0, tiled=True)[0]
    return out, relocate(own, old_owner, new_owner)[None]


def solution(mesh):
    fine = Mesh(mesh.devices.reshape(4, 4, 2, 2, mesh.shape["mp"]), ("y", "x", "zh", "c", "mp"))
    expert = ("y", "x", "zh", "c")
    in_specs = (
        P(expert, None),
        P(expert, None),
        P(expert, None),
        P(expert, None, None, "mp"),
        P(),
        P(),
    )
    out_specs = (P(expert, "mp"), P(expert, None, None, "mp"))
    return jax.shard_map(shards, mesh=fine, in_specs=in_specs, out_specs=out_specs, check_vma=False)
```

```python
import jax
import jax.numpy as jnp
from jax import lax
from jax.sharding import Mesh, PartitionSpec as P

PLANE = ("y", "x", "c")
NEAR = ("mb", "mc")
CAP = 16


def swap(value, axis):
    return lax.ppermute(value, axis, [(0, 1), (1, 0)])


def place_codes(routes, gate_values, owner):
    experts = owner.shape[0]
    flat = routes.T.reshape(-1)
    count = flat.shape[0]
    ids = jnp.arange(experts, dtype=jnp.int32)
    hot = (flat[:, None] == ids[None, :]).astype(jnp.bfloat16)
    at = jnp.arange(count, dtype=jnp.int32)
    earlier = (at[:, None] > at[None, :]).astype(jnp.bfloat16)
    before = jnp.dot(earlier, hot, preferred_element_type=jnp.float32)
    code = jnp.sum(hot.astype(jnp.float32) * (before + (owner * CAP).astype(jnp.float32)[None, :]), axis=1)
    return jnp.concatenate([code.reshape(routes.shape[1], -1), gate_values.T], axis=0)


def placed_rows(codes, zh):
    code = codes[:2].astype(jnp.int32)
    slot, rank = code // CAP, code % CAP
    row = jnp.where(slot % 2 == zh, (slot // 2) * (2 * CAP) + rank, -2 * CAP)
    return jnp.stack([row, row + CAP], axis=1).reshape(2, -1)


def plane_rows():
    return 2 * CAP * lax.axis_size("y") * lax.axis_size("x")


def gather_rows(rows, table):
    at = jnp.arange(plane_rows(), dtype=jnp.int32)
    pick = ((rows[0][None, :] == at[:, None]) | (rows[1][None, :] == at[:, None])).astype(jnp.bfloat16)
    return jnp.dot(pick, table, preferred_element_type=jnp.float32).astype(jnp.bfloat16)


def exchange(rows, axes=PLANE):
    blocks = rows.reshape((lax.axis_size(axes), -1, rows.shape[-1]))
    return lax.all_to_all(blocks, axes, split_axis=0, concat_axis=0, tiled=True).reshape(rows.shape)


def expert_part(rows, weights):
    half = jnp.einsum("rd,gdf->grf", rows, weights[:2], preferred_element_type=jnp.float32)
    total = half + swap(half, "c")
    hidden = (jax.nn.silu(total[0]) * total[1]).astype(jnp.bfloat16)
    return lax.dot_general(
        hidden, weights[2], (((1,), (1,)), ((), ())), preferred_element_type=jnp.float32
    ).astype(jnp.bfloat16)


def weighted(back, codes, rows):
    at = jnp.arange(back.shape[0], dtype=jnp.int32)
    gate = jnp.concatenate([codes[2:4], codes[2:4]], axis=1)
    mix = sum(jnp.where(rows[k][:, None] == at[None, :], gate[k][:, None], 0.0) for k in range(2))
    high = mix.astype(jnp.bfloat16)
    low = (mix - high.astype(jnp.float32)).astype(jnp.bfloat16)
    return jnp.dot(high, back, preferred_element_type=jnp.float32) + jnp.dot(
        low, back, preferred_element_type=jnp.float32
    )


def by_columns(mixed, near):
    tok_rows = mixed.shape[0] // 2
    parts = mixed.astype(jnp.bfloat16).reshape(2, tok_rows, 2, near, -1)
    return jnp.transpose(parts, (3, 2, 1, 0, 4)).reshape(near, 2, tok_rows, -1)


def near_sum(parts, place):
    total = lax.dynamic_index_in_dim(parts, place, 0, keepdims=False).astype(jnp.float32)
    count = parts.shape[0]
    for step in range(1, count):
        block = lax.dynamic_index_in_dim(parts, place ^ step, 0, keepdims=False)
        total += lax.ppermute(block, NEAR, [(i, i ^ step) for i in range(count)]).astype(jnp.float32)
    return total


def after(value, *others):
    return lax.optimization_barrier((value, *others))[0]


def pick_pieces(spread, old_owner, new_owner, zh):
    moved = new_owner != old_owner
    low = jnp.min(jnp.where(moved, old_owner, old_owner.shape[0]))
    high = jnp.max(jnp.where(moved, old_owner, -1))
    low_piece = lax.dynamic_index_in_dim(spread, low >> 1, 0, keepdims=False)
    high_piece = lax.dynamic_index_in_dim(spread, high >> 1, 0, keepdims=False)
    low_here, high_here = (low & 1) == zh, (high & 1) == zh
    other = swap(jnp.where(low_here, low_piece, high_piece), "zh")
    to_low = jnp.where(high_here, high_piece, other)
    to_high = jnp.where(low_here, low_piece, other)
    slots = 2 * jnp.arange(spread.shape[0], dtype=jnp.int32)[:, None, None] + zh
    return jnp.where(slots == low, to_low[None], jnp.where(slots == high, to_high[None], spread))


def shards(tokens, routes, gate_values, expert_weights, old_owner, new_owner):
    zh, far, place = lax.axis_index("zh"), lax.axis_index("ma"), lax.axis_index(NEAR)
    near = lax.axis_size(NEAR)
    tok_rows = tokens.shape[0]
    own = expert_weights[0]
    table = jnp.transpose(tokens.reshape(tok_rows, 2 * near, 2, -1), (2, 0, 1, 3)).reshape(2 * tok_rows, -1)
    share = 2 * tok_rows // near
    quarter = swap(lax.dynamic_slice_in_dim(table, place * share, share, 0), "zh")
    codes = place_codes(routes, gate_values, old_owner)
    other_codes = swap(codes, "zh")
    other_table = lax.all_gather(quarter, NEAR, tiled=True)

    chips = lax.axis_size("y") * lax.axis_size("x")
    pieces = own.reshape(chips, -1, own.shape[-1])
    spread = lax.all_to_all(pieces, ("y", "x"), split_axis=0, concat_axis=0, tiled=True)
    rows = placed_rows(codes, zh)
    sent = exchange(after(gather_rows(rows, table), spread, quarter, other_codes))
    other_rows = placed_rows(other_codes, zh)
    other_sent = exchange(after(gather_rows(other_rows, other_table), sent))
    back = exchange(after(expert_part(sent, own), other_sent))
    other_back = exchange(after(expert_part(other_sent, own), back))

    parts = by_columns(weighted(back, codes, rows), near)
    kept = lax.psum_scatter(parts, NEAR, scatter_dimension=0, tiled=True)[0]
    other_parts = by_columns(weighted(other_back, other_codes, other_rows), near)
    chosen = pick_pieces(spread, old_owner, new_owner, zh)
    arrived = lax.all_to_all(after(chosen, other_back), ("y", "x"), split_axis=0, concat_axis=0, tiled=True)
    other_kept = near_sum(other_parts, place).astype(jnp.bfloat16)

    def of(value, index):
        return lax.dynamic_index_in_dim(value, index, 0, keepdims=False)

    total = of(kept, far).astype(jnp.float32)
    total += swap(of(kept, 1 - far), "ma").astype(jnp.float32)
    total += swap(of(other_kept, far), "zh").astype(jnp.float32)
    total += lax.ppermute(of(other_kept, 1 - far), ("zh", "ma"), [(i, i ^ 3) for i in range(4)]).astype(jnp.float32)
    return total.astype(jnp.bfloat16), arrived.reshape(expert_weights.shape)


def solution(mesh):
    fine = Mesh(mesh.devices.reshape(4, 4, 2, 2, 2, 2, 2), ("y", "x", "zh", "c", "ma", "mb", "mc"))
    expert, mp = ("y", "x", "zh", "c"), ("ma", "mb", "mc")
    in_specs = (
        P(expert, None),
        P(expert, None),
        P(expert, None),
        P(expert, None, None, mp),
        P(),
        P(),
    )
    out_specs = (P(expert, mp), P(expert, None, None, mp))
    return jax.shard_map(shards, mesh=fine, in_specs=in_specs, out_specs=out_specs, check_vma=False)
```

```python
import jax
import jax.numpy as jnp
from jax import lax
from jax.sharding import Mesh, PartitionSpec as P

PLANE = ("y", "x", "c")
RING = ("zh", "mp")
CAP = 16


def swap(value, axis):
    return lax.ppermute(value, axis, [(0, 1), (1, 0)])


def place_codes(routes, gate_values, owner):
    experts = owner.shape[0]
    flat = routes.T.reshape(-1)
    count = flat.shape[0]
    ids = jnp.arange(experts, dtype=jnp.int32)
    hot = (flat[:, None] == ids[None, :]).astype(jnp.bfloat16)
    at = jnp.arange(count, dtype=jnp.int32)
    earlier = (at[:, None] > at[None, :]).astype(jnp.bfloat16)
    before = jnp.dot(earlier, hot, preferred_element_type=jnp.float32)
    code = jnp.sum(hot.astype(jnp.float32) * (before + (owner * CAP).astype(jnp.float32)[None, :]), axis=1)
    return jnp.concatenate([code.reshape(routes.shape[1], -1), gate_values.T], axis=0)


def placed_rows(codes, zh):
    code = codes[:2].astype(jnp.int32)
    slot, rank = code // CAP, code % CAP
    row = jnp.where(slot % 2 == zh, (slot // 2) * (2 * CAP) + rank, -2 * CAP)
    return jnp.stack([row, row + CAP], axis=1).reshape(2, -1)


def plane_rows():
    return 2 * CAP * lax.axis_size("y") * lax.axis_size("x")


def gather_rows(rows, table):
    at = jnp.arange(plane_rows(), dtype=jnp.int32)
    pick = ((rows[0][None, :] == at[:, None]) | (rows[1][None, :] == at[:, None])).astype(jnp.bfloat16)
    return jnp.dot(pick, table, preferred_element_type=jnp.float32).astype(jnp.bfloat16)


def exchange(rows, axes=PLANE):
    blocks = rows.reshape((lax.axis_size(axes), -1, rows.shape[-1]))
    return lax.all_to_all(blocks, axes, split_axis=0, concat_axis=0, tiled=True).reshape(rows.shape)


def expert_part(rows, weights):
    half = jnp.einsum("rd,gdf->grf", rows, weights[:2], preferred_element_type=jnp.float32)
    total = half + swap(half, "c")
    hidden = (jax.nn.silu(total[0]) * total[1]).astype(jnp.bfloat16)
    return lax.dot_general(
        hidden, weights[2], (((1,), (1,)), ((), ())), preferred_element_type=jnp.float32
    ).astype(jnp.bfloat16)


def weighted(back, codes, rows):
    at = jnp.arange(back.shape[0], dtype=jnp.int32)
    gate = jnp.concatenate([codes[2:4], codes[2:4]], axis=1)
    mix = sum(jnp.where(rows[k][:, None] == at[None, :], gate[k][:, None], 0.0) for k in range(2))
    high = mix.astype(jnp.bfloat16)
    low = (mix - high.astype(jnp.float32)).astype(jnp.bfloat16)
    return jnp.dot(high, back, preferred_element_type=jnp.float32) + jnp.dot(
        low, back, preferred_element_type=jnp.float32
    )


def by_columns(mixed, groups):
    parts = mixed.astype(jnp.bfloat16).reshape(2, mixed.shape[0] // 2, groups, -1)
    return jnp.transpose(parts, (2, 1, 0, 3)).reshape(groups, mixed.shape[0] // 2, -1)


def after(value, *others):
    return lax.optimization_barrier((value, *others))[0]


def pick_pieces(spread, old_owner, new_owner, zh):
    moved = new_owner != old_owner
    low = jnp.min(jnp.where(moved, old_owner, old_owner.shape[0]))
    high = jnp.max(jnp.where(moved, old_owner, -1))
    low_piece = lax.dynamic_index_in_dim(spread, low >> 1, 0, keepdims=False)
    high_piece = lax.dynamic_index_in_dim(spread, high >> 1, 0, keepdims=False)
    low_here, high_here = (low & 1) == zh, (high & 1) == zh
    other = swap(jnp.where(low_here, low_piece, high_piece), "zh")
    to_low = jnp.where(high_here, high_piece, other)
    to_high = jnp.where(low_here, low_piece, other)
    slots = 2 * jnp.arange(spread.shape[0], dtype=jnp.int32)[:, None, None] + zh
    return jnp.where(slots == low, to_low[None], jnp.where(slots == high, to_high[None], spread))


def shards(tokens, routes, gate_values, expert_weights, old_owner, new_owner):
    zh, lane = lax.axis_index("zh"), lax.axis_index("mp")
    groups = lax.axis_size("mp")
    tok_rows, width = tokens.shape
    own = expert_weights[0]
    codes = place_codes(routes, gate_values, old_owner)
    other_codes = swap(codes, "zh")
    table = jnp.transpose(tokens.reshape(tok_rows, groups, 2, -1), (2, 0, 1, 3)).reshape(2 * tok_rows, -1)
    share = 2 * tok_rows // groups
    part = lax.dynamic_slice_in_dim(table, lane * share, share, 0)
    ring = lax.all_gather(part, RING)
    rows, other_rows = placed_rows(codes, zh), placed_rows(other_codes, zh)
    back = exchange(expert_part(exchange(after(gather_rows(rows, table), part)), own))

    ring = after(ring, back)
    other_table = lax.dynamic_slice_in_dim(ring, (1 - zh) * groups, groups, 0).reshape(2 * tok_rows, -1)
    other_sent = exchange(gather_rows(other_rows, other_table))
    mixed = by_columns(weighted(back, codes, rows), groups)
    both = jnp.zeros((2 * groups,) + mixed.shape[1:], mixed.dtype)
    both = lax.dynamic_update_slice_in_dim(both, mixed, zh * groups, 0)
    both, other_sent = lax.optimization_barrier((both, other_sent))
    other_back = exchange(expert_part(other_sent, own))
    other_mixed = by_columns(weighted(other_back, other_codes, other_rows), groups)
    both = lax.dynamic_update_slice_in_dim(both, other_mixed, (1 - zh) * groups, 0)
    out = lax.psum_scatter(both, RING, scatter_dimension=0, tiled=True)[0]

    plane = ("y", "x")
    pieces = own.reshape(lax.axis_size(plane), -1, own.shape[-1])
    spread = lax.all_to_all(after(pieces, other_back), plane, split_axis=0, concat_axis=0, tiled=True)
    chosen = pick_pieces(spread, old_owner, new_owner, zh)
    arrived = lax.all_to_all(chosen, plane, split_axis=0, concat_axis=0, tiled=True)
    return out, arrived.reshape(expert_weights.shape)


def solution(mesh):
    fine = Mesh(mesh.devices.reshape(4, 4, 2, 2, mesh.shape["mp"]), ("y", "x", "zh", "c", "mp"))
    expert = ("y", "x", "zh", "c")
    in_specs = (
        P(expert, None),
        P(expert, None),
        P(expert, None),
        P(expert, None, None, "mp"),
        P(),
        P(),
    )
    out_specs = (P(expert, "mp"), P(expert, None, None, "mp"))
    return jax.shard_map(shards, mesh=fine, in_specs=in_specs, out_specs=out_specs, check_vma=False)
```

```python
import jax
import jax.numpy as jnp
from jax import lax
from jax.sharding import Mesh, PartitionSpec as P

PLANE = ("y", "x", "c")
NEAR = ("mb", "mc")
CAP = 16


def swap(value, axis):
    return lax.ppermute(value, axis, [(0, 1), (1, 0)])


def place_codes(routes, gate_values, owner):
    experts = owner.shape[0]
    flat = routes.T.reshape(-1)
    count = flat.shape[0]
    ids = jnp.arange(experts, dtype=jnp.int32)
    hot = (flat[:, None] == ids[None, :]).astype(jnp.bfloat16)
    at = jnp.arange(count, dtype=jnp.int32)
    earlier = (at[:, None] > at[None, :]).astype(jnp.bfloat16)
    before = jnp.dot(earlier, hot, preferred_element_type=jnp.float32)
    code = jnp.sum(hot.astype(jnp.float32) * (before + (owner * CAP).astype(jnp.float32)[None, :]), axis=1)
    return jnp.concatenate([code.reshape(routes.shape[1], -1), gate_values.T], axis=0)


def placed_rows(codes, zh):
    code = codes[:2].astype(jnp.int32)
    slot, rank = code // CAP, code % CAP
    row = jnp.where(slot % 2 == zh, (slot // 2) * (2 * CAP) + rank, -2 * CAP)
    return jnp.stack([row, row + CAP], axis=1).reshape(2, -1)


def plane_rows():
    return 2 * CAP * lax.axis_size("y") * lax.axis_size("x")


def gather_rows(rows, table):
    at = jnp.arange(plane_rows(), dtype=jnp.int32)
    pick = ((rows[0][None, :] == at[:, None]) | (rows[1][None, :] == at[:, None])).astype(jnp.bfloat16)
    return jnp.dot(pick, table, preferred_element_type=jnp.float32).astype(jnp.bfloat16)


def exchange(rows, axes=PLANE):
    blocks = rows.reshape((lax.axis_size(axes), -1, rows.shape[-1]))
    return lax.all_to_all(blocks, axes, split_axis=0, concat_axis=0, tiled=True).reshape(rows.shape)


def expert_part(rows, weights):
    half = jnp.einsum("rd,gdf->grf", rows, weights[:2], preferred_element_type=jnp.float32)
    total = half + swap(half, "c")
    hidden = (jax.nn.silu(total[0]) * total[1]).astype(jnp.bfloat16)
    return lax.dot_general(
        hidden, weights[2], (((1,), (1,)), ((), ())), preferred_element_type=jnp.float32
    ).astype(jnp.bfloat16)


def weighted(back, codes, rows):
    at = jnp.arange(back.shape[0], dtype=jnp.int32)
    gate = jnp.concatenate([codes[2:4], codes[2:4]], axis=1)
    mix = sum(jnp.where(rows[k][:, None] == at[None, :], gate[k][:, None], 0.0) for k in range(2))
    high = mix.astype(jnp.bfloat16)
    low = (mix - high.astype(jnp.float32)).astype(jnp.bfloat16)
    return jnp.dot(high, back, preferred_element_type=jnp.float32) + jnp.dot(
        low, back, preferred_element_type=jnp.float32
    )


def by_columns(mixed, near):
    tok_rows = mixed.shape[0] // 2
    parts = mixed.astype(jnp.bfloat16).reshape(2, tok_rows, 2, near, -1)
    return jnp.transpose(parts, (3, 2, 1, 0, 4)).reshape(near, 2, tok_rows, -1)


def near_sum(parts, place):
    total = lax.dynamic_index_in_dim(parts, place, 0, keepdims=False).astype(jnp.float32)
    count = parts.shape[0]
    for step in range(1, count):
        block = lax.dynamic_index_in_dim(parts, place ^ step, 0, keepdims=False)
        total += lax.ppermute(block, NEAR, [(i, i ^ step) for i in range(count)]).astype(jnp.float32)
    return total


tied = lax.optimization_barrier


def pick_pieces(spread, old_owner, new_owner, zh):
    moved = new_owner != old_owner
    low = jnp.min(jnp.where(moved, old_owner, old_owner.shape[0]))
    high = jnp.max(jnp.where(moved, old_owner, -1))
    low_piece = lax.dynamic_index_in_dim(spread, low >> 1, 0, keepdims=False)
    high_piece = lax.dynamic_index_in_dim(spread, high >> 1, 0, keepdims=False)
    low_here, high_here = (low & 1) == zh, (high & 1) == zh
    other = swap(jnp.where(low_here, low_piece, high_piece), "zh")
    to_low = jnp.where(high_here, high_piece, other)
    to_high = jnp.where(low_here, low_piece, other)
    slots = 2 * jnp.arange(spread.shape[0], dtype=jnp.int32)[:, None, None] + zh
    return jnp.where(slots == low, to_low[None], jnp.where(slots == high, to_high[None], spread))


def shards(tokens, routes, gate_values, expert_weights, old_owner, new_owner):
    zh, far, place = lax.axis_index("zh"), lax.axis_index("ma"), lax.axis_index(NEAR)
    near = lax.axis_size(NEAR)
    tok_rows = tokens.shape[0]
    own = expert_weights[0]
    table = jnp.transpose(tokens.reshape(tok_rows, 2 * near, 2, -1), (2, 0, 1, 3)).reshape(2 * tok_rows, -1)
    share = 2 * tok_rows // near
    part = lax.dynamic_slice_in_dim(table, place * share, share, 0)
    codes = place_codes(routes, gate_values, old_owner)
    rows = placed_rows(codes, zh)
    part, payload = tied((part, gather_rows(rows, table)))
    quarter = swap(part, "zh")
    sent = exchange(payload)
    chips = lax.axis_size("y") * lax.axis_size("x")
    pieces, sent, quarter = tied((own.reshape(chips, -1, own.shape[-1]), sent, quarter))
    spread = lax.all_to_all(pieces, ("y", "x"), split_axis=0, concat_axis=0, tiled=True)
    quarter, later_codes = tied((quarter, codes))
    other_codes = swap(later_codes, "zh")
    other_rows = placed_rows(other_codes, zh)
    other_table = lax.all_gather(quarter, NEAR, tiled=True)
    payload, spread = tied((gather_rows(other_rows, other_table), spread))
    other_sent = exchange(payload)
    payload, other_sent = tied((expert_part(sent, own), other_sent))
    back = exchange(payload)
    chosen = pick_pieces(spread, old_owner, new_owner, zh)
    payload, back, chosen = tied((expert_part(other_sent, own), back, chosen))
    other_back = exchange(payload)

    parts = by_columns(weighted(back, codes, rows), near)
    kept = near_sum(parts, place).astype(jnp.bfloat16)
    other_back, kept = tied((other_back, kept))
    other_parts = by_columns(weighted(other_back, other_codes, other_rows), near)
    near_parts = lax.all_to_all(other_parts, NEAR, split_axis=0, concat_axis=0, tiled=True)
    near_parts, chosen = tied((near_parts, chosen))
    arrived = lax.all_to_all(chosen, ("y", "x"), split_axis=0, concat_axis=0, tiled=True)
    other_kept = jnp.sum(near_parts.astype(jnp.float32), axis=0).astype(jnp.bfloat16)

    def of(value, index):
        return lax.dynamic_index_in_dim(value, index, 0, keepdims=False)

    total = of(kept, far).astype(jnp.float32)
    total += swap(of(kept, 1 - far), "ma").astype(jnp.float32)
    total += swap(of(other_kept, far), "zh").astype(jnp.float32)
    total += lax.ppermute(of(other_kept, 1 - far), ("zh", "ma"), [(i, i ^ 3) for i in range(4)]).astype(jnp.float32)
    return total.astype(jnp.bfloat16), arrived.reshape(expert_weights.shape)


def solution(mesh):
    fine = Mesh(mesh.devices.reshape(4, 4, 2, 2, 2, 2, 2), ("y", "x", "zh", "c", "ma", "mb", "mc"))
    expert, mp = ("y", "x", "zh", "c"), ("ma", "mb", "mc")
    in_specs = (
        P(expert, None),
        P(expert, None),
        P(expert, None),
        P(expert, None, None, mp),
        P(),
        P(),
    )
    out_specs = (P(expert, mp), P(expert, None, None, mp))
    return jax.shard_map(shards, mesh=fine, in_specs=in_specs, out_specs=out_specs, check_vma=False)
```

```python
import jax
import jax.numpy as jnp
from jax import lax
from jax.sharding import Mesh, PartitionSpec as P

PLANE = ("y", "x", "c")
NEAR = ("mb", "mc")
RING = ("zh", "ma", "mb", "mc")
CAP = 16


def swap(value, axis):
    return lax.ppermute(value, axis, [(0, 1), (1, 0)])


def mirrored(value):
    return lax.ppermute(value, RING, [(i, 15 - i) for i in range(16)])


def place_codes(routes, gate_values, owner):
    experts = owner.shape[0]
    flat = routes.T.reshape(-1)
    count = flat.shape[0]
    ids = jnp.arange(experts, dtype=jnp.int32)
    hot = (flat[:, None] == ids[None, :]).astype(jnp.bfloat16)
    at = jnp.arange(count, dtype=jnp.int32)
    earlier = (at[:, None] > at[None, :]).astype(jnp.bfloat16)
    before = jnp.dot(earlier, hot, preferred_element_type=jnp.float32)
    code = jnp.sum(hot.astype(jnp.float32) * (before + (owner * CAP).astype(jnp.float32)[None, :]), axis=1)
    return jnp.concatenate([code.reshape(routes.shape[1], -1), gate_values.T], axis=0)


def placed_rows(codes, zh):
    code = codes[:2].astype(jnp.int32)
    slot, rank = code // CAP, code % CAP
    row = jnp.where(slot % 2 == zh, (slot // 2) * (2 * CAP) + rank, -2 * CAP)
    return jnp.stack([row, row + CAP], axis=1).reshape(2, -1)


def plane_rows():
    return 2 * CAP * lax.axis_size("y") * lax.axis_size("x")


def gather_rows(rows, table):
    at = jnp.arange(plane_rows(), dtype=jnp.int32)
    pick = ((rows[0][None, :] == at[:, None]) | (rows[1][None, :] == at[:, None])).astype(jnp.bfloat16)
    return jnp.dot(pick, table, preferred_element_type=jnp.float32).astype(jnp.bfloat16)


def exchange(rows, axes=PLANE):
    blocks = rows.reshape((lax.axis_size(axes), -1, rows.shape[-1]))
    return lax.all_to_all(blocks, axes, split_axis=0, concat_axis=0, tiled=True).reshape(rows.shape)


def expert_part(rows, weights):
    half = jnp.einsum("rd,gdf->grf", rows, weights[:2], preferred_element_type=jnp.float32)
    total = half + swap(half, "c")
    hidden = (jax.nn.silu(total[0]) * total[1]).astype(jnp.bfloat16)
    return lax.dot_general(
        hidden, weights[2], (((1,), (1,)), ((), ())), preferred_element_type=jnp.float32
    ).astype(jnp.bfloat16)


def weighted(back, codes, rows):
    at = jnp.arange(back.shape[0], dtype=jnp.int32)
    gate = jnp.concatenate([codes[2:4], codes[2:4]], axis=1)
    mix = sum(jnp.where(rows[k][:, None] == at[None, :], gate[k][:, None], 0.0) for k in range(2))
    high = mix.astype(jnp.bfloat16)
    low = (mix - high.astype(jnp.float32)).astype(jnp.bfloat16)
    return jnp.dot(high, back, preferred_element_type=jnp.float32) + jnp.dot(
        low, back, preferred_element_type=jnp.float32
    )


def by_columns(mixed, groups):
    parts = mixed.astype(jnp.bfloat16).reshape(2, mixed.shape[0] // 2, groups, -1)
    return jnp.transpose(parts, (2, 1, 0, 3)).reshape(groups, mixed.shape[0] // 2, -1)


tied = lax.optimization_barrier


def pick_pieces(spread, old_owner, new_owner, zh):
    moved = new_owner != old_owner
    low = jnp.min(jnp.where(moved, old_owner, old_owner.shape[0]))
    high = jnp.max(jnp.where(moved, old_owner, -1))
    low_piece = lax.dynamic_index_in_dim(spread, low >> 1, 0, keepdims=False)
    high_piece = lax.dynamic_index_in_dim(spread, high >> 1, 0, keepdims=False)
    low_here, high_here = (low & 1) == zh, (high & 1) == zh
    other = swap(jnp.where(low_here, low_piece, high_piece), "zh")
    to_low = jnp.where(high_here, high_piece, other)
    to_high = jnp.where(low_here, low_piece, other)
    slots = 2 * jnp.arange(spread.shape[0], dtype=jnp.int32)[:, None, None] + zh
    return jnp.where(slots == low, to_low[None], jnp.where(slots == high, to_high[None], spread))


def shards(tokens, routes, gate_values, expert_weights, old_owner, new_owner):
    zh, place = lax.axis_index("zh"), lax.axis_index(NEAR)
    near = lax.axis_size(NEAR)
    tok_rows = tokens.shape[0]
    own = expert_weights[0]
    table = jnp.transpose(tokens.reshape(tok_rows, 2 * near, 2, -1), (2, 0, 1, 3)).reshape(2 * tok_rows, -1)
    share = 2 * tok_rows // near
    part = lax.dynamic_slice_in_dim(table, (near - 1 - place) * share, share, 0)
    codes = place_codes(routes, gate_values, old_owner)
    rows = placed_rows(codes, zh)
    part, payload = tied((part, gather_rows(rows, table)))
    quarter = mirrored(part)
    sent = exchange(payload)
    sent, quarter = tied((sent, quarter))
    quarter, payload, later_codes = tied((quarter, expert_part(sent, own), codes))
    back = exchange(payload)
    other_codes = mirrored(later_codes)
    other_rows = placed_rows(other_codes, zh)
    other_table = lax.all_gather(quarter, NEAR, tiled=True)
    payload, back = tied((gather_rows(other_rows, other_table), back))
    other_sent = exchange(payload)

    mixed = by_columns(weighted(back, codes, rows), 2 * near)
    both = jnp.zeros((4 * near,) + mixed.shape[1:], mixed.dtype)
    both = lax.dynamic_update_slice_in_dim(both, mixed, zh * 2 * near, 0)
    both, other_sent = tied((both, other_sent))
    other_back = exchange(expert_part(other_sent, own))
    chips = lax.axis_size("y") * lax.axis_size("x")
    pieces, other_back = tied((own.reshape(chips, -1, own.shape[-1]), other_back))
    spread = lax.all_to_all(pieces, ("y", "x"), split_axis=0, concat_axis=0, tiled=True)
    other_mixed = by_columns(weighted(other_back, other_codes, other_rows), 2 * near)
    both = lax.dynamic_update_slice_in_dim(both, other_mixed, (1 - zh) * 2 * near, 0)
    out = lax.psum_scatter(both, RING, scatter_dimension=0, tiled=True)[0]
    chosen = pick_pieces(spread, old_owner, new_owner, zh)
    arrived = lax.all_to_all(chosen, ("y", "x"), split_axis=0, concat_axis=0, tiled=True)
    return out, arrived.reshape(expert_weights.shape)


def solution(mesh):
    fine = Mesh(mesh.devices.reshape(4, 4, 2, 2, 2, 2, 2), ("y", "x", "zh", "c", "ma", "mb", "mc"))
    expert, mp = ("y", "x", "zh", "c"), ("ma", "mb", "mc")
    in_specs = (
        P(expert, None),
        P(expert, None),
        P(expert, None),
        P(expert, None, None, mp),
        P(),
        P(),
    )
    out_specs = (P(expert, mp), P(expert, None, None, mp))
    return jax.shard_map(shards, mesh=fine, in_specs=in_specs, out_specs=out_specs, check_vma=False)
```

```python
import jax
import jax.numpy as jnp
from jax import lax
from jax.experimental.layout import Layout, with_layout_constraint
from jax.sharding import Mesh, PartitionSpec as P

PLANE = ("y", "x", "c")
NEAR = ("mb", "mc")
RING = ("zh", "ma", "mb", "mc")
CAP = 16


def swap(value, axis):
    return lax.ppermute(value, axis, [(0, 1), (1, 0)])


def mirrored(value):
    return lax.ppermute(value, RING, [(i, 15 - i) for i in range(16)])


def place_codes(routes, gate_values, owner):
    experts = owner.shape[0]
    flat = routes.T.reshape(-1)
    count = flat.shape[0]
    ids = jnp.arange(experts, dtype=jnp.int32)
    hot = (flat[:, None] == ids[None, :]).astype(jnp.bfloat16)
    at = jnp.arange(count, dtype=jnp.int32)
    earlier = (at[:, None] > at[None, :]).astype(jnp.bfloat16)
    before = jnp.dot(earlier, hot, preferred_element_type=jnp.float32)
    code = jnp.sum(hot.astype(jnp.float32) * (before + (owner * CAP).astype(jnp.float32)[None, :]), axis=1)
    return jnp.concatenate([code.reshape(routes.shape[1], -1), gate_values.T], axis=0)


def placed_rows(codes, zh):
    code = codes[:2].astype(jnp.int32)
    slot, rank = code // CAP, code % CAP
    row = jnp.where(slot % 2 == zh, (slot // 2) * (2 * CAP) + rank, -2 * CAP)
    return jnp.stack([row, row + CAP], axis=1).reshape(2, -1)


def plane_rows():
    return 2 * CAP * lax.axis_size("y") * lax.axis_size("x")


def gather_rows(rows, table):
    at = jnp.arange(plane_rows(), dtype=jnp.int32)
    pick = ((rows[0][None, :] == at[:, None]) | (rows[1][None, :] == at[:, None])).astype(jnp.bfloat16)
    return jnp.dot(pick, table, preferred_element_type=jnp.float32).astype(jnp.bfloat16)


def exchange(rows, axes=PLANE):
    blocks = rows.reshape((lax.axis_size(axes), -1, rows.shape[-1]))
    return lax.all_to_all(blocks, axes, split_axis=0, concat_axis=0, tiled=True).reshape(rows.shape)


def expert_part(rows, weights):
    half = jnp.einsum("rd,gdf->grf", rows, weights[:2], preferred_element_type=jnp.float32)
    total = half + swap(half, "c")
    hidden = (jax.nn.silu(total[0]) * total[1]).astype(jnp.bfloat16)
    return lax.dot_general(
        hidden, weights[2], (((1,), (1,)), ((), ())), preferred_element_type=jnp.float32
    ).astype(jnp.bfloat16)


def weighted(back, codes, rows):
    at = jnp.arange(back.shape[0], dtype=jnp.int32)
    gate = jnp.concatenate([codes[2:4], codes[2:4]], axis=1)
    mix = sum(jnp.where(rows[k][:, None] == at[None, :], gate[k][:, None], 0.0) for k in range(2))
    high = mix.astype(jnp.bfloat16)
    low = (mix - high.astype(jnp.float32)).astype(jnp.bfloat16)
    return jnp.dot(high, back, preferred_element_type=jnp.float32) + jnp.dot(
        low, back, preferred_element_type=jnp.float32
    )


def by_columns(mixed, groups):
    parts = mixed.astype(jnp.bfloat16).reshape(2, mixed.shape[0] // 2, groups, -1)
    return jnp.transpose(parts, (2, 1, 0, 3)).reshape(groups, mixed.shape[0] // 2, -1)


tied = lax.optimization_barrier


def pick_pieces(spread, old_owner, new_owner, zh):
    moved = new_owner != old_owner
    low = jnp.min(jnp.where(moved, old_owner, old_owner.shape[0]))
    high = jnp.max(jnp.where(moved, old_owner, -1))
    low_piece = lax.dynamic_index_in_dim(spread, low >> 1, 0, keepdims=False)
    high_piece = lax.dynamic_index_in_dim(spread, high >> 1, 0, keepdims=False)
    low_here, high_here = (low & 1) == zh, (high & 1) == zh
    other = swap(jnp.where(low_here, low_piece, high_piece), "zh")
    to_low = jnp.where(high_here, high_piece, other)
    to_high = jnp.where(low_here, low_piece, other)
    slots = 2 * jnp.arange(spread.shape[0], dtype=jnp.int32)[:, None, None] + zh
    return jnp.where(slots == low, to_low[None], jnp.where(slots == high, to_high[None], spread))


def shards(tokens, routes, gate_values, expert_weights, old_owner, new_owner):
    zh, place = lax.axis_index("zh"), lax.axis_index(NEAR)
    near = lax.axis_size(NEAR)
    tok_rows = tokens.shape[0]
    own = expert_weights[0]
    table = jnp.transpose(tokens.reshape(tok_rows, 2 * near, 2, -1), (2, 0, 1, 3)).reshape(2 * tok_rows, -1)
    table = with_layout_constraint(table, Layout(major_to_minor=(0, 1)))
    share = 2 * tok_rows // near
    part = lax.dynamic_slice_in_dim(table, (near - 1 - place) * share, share, 0)
    codes = place_codes(routes, gate_values, old_owner)
    rows = placed_rows(codes, zh)
    part, payload = tied((part, gather_rows(rows, table)))
    quarter = mirrored(part)
    sent = exchange(payload)
    sent, quarter = tied((sent, quarter))
    quarter, payload, later_codes = tied((quarter, expert_part(sent, own), codes))
    back = exchange(payload)
    other_codes = mirrored(later_codes)
    other_rows = placed_rows(other_codes, zh)
    other_table = lax.all_gather(quarter, NEAR, tiled=True)
    payload, back = tied((gather_rows(other_rows, other_table), back))
    other_sent = exchange(payload)

    mixed = by_columns(weighted(back, codes, rows), 2 * near)
    both = jnp.zeros((4 * near,) + mixed.shape[1:], mixed.dtype)
    both = lax.dynamic_update_slice_in_dim(both, mixed, zh * 2 * near, 0)
    both, other_sent = tied((both, other_sent))
    other_back = exchange(expert_part(other_sent, own))
    chips = lax.axis_size("y") * lax.axis_size("x")
    pieces, other_back = tied((own.reshape(chips, -1, own.shape[-1]), other_back))
    spread = lax.all_to_all(pieces, ("y", "x"), split_axis=0, concat_axis=0, tiled=True)
    other_mixed = by_columns(weighted(other_back, other_codes, other_rows), 2 * near)
    both = lax.dynamic_update_slice_in_dim(both, other_mixed, (1 - zh) * 2 * near, 0)
    out = lax.psum_scatter(both, RING, scatter_dimension=0, tiled=True)[0]
    chosen = pick_pieces(spread, old_owner, new_owner, zh)
    arrived = lax.all_to_all(chosen, ("y", "x"), split_axis=0, concat_axis=0, tiled=True)
    return out, arrived.reshape(expert_weights.shape)


def solution(mesh):
    fine = Mesh(mesh.devices.reshape(4, 4, 2, 2, 2, 2, 2), ("y", "x", "zh", "c", "ma", "mb", "mc"))
    expert, mp = ("y", "x", "zh", "c"), ("ma", "mb", "mc")
    in_specs = (
        P(expert, None),
        P(expert, None),
        P(expert, None),
        P(expert, None, None, mp),
        P(),
        P(),
    )
    out_specs = (P(expert, mp), P(expert, None, None, mp))
    return jax.shard_map(shards, mesh=fine, in_specs=in_specs, out_specs=out_specs, check_vma=False)
```

```python
import jax
import jax.numpy as jnp
from jax import lax
from jax.experimental.layout import Layout, with_layout_constraint
from jax.sharding import Mesh, PartitionSpec as P

PLANE = ("y", "x", "c")
NEAR = ("mb", "mc")
RING = ("zh", "ma", "mb", "mc")
CAP = 16


def swap(value, axis):
    return lax.ppermute(value, axis, [(0, 1), (1, 0)])


def mirrored(value):
    return lax.ppermute(value, RING, [(i, 15 - i) for i in range(16)])


def place_codes(routes, gate_values, owner):
    experts = owner.shape[0]
    flat = routes.T.reshape(-1)
    count = flat.shape[0]
    ids = jnp.arange(experts, dtype=jnp.int32)
    hot = (flat[:, None] == ids[None, :]).astype(jnp.bfloat16)
    at = jnp.arange(count, dtype=jnp.int32)
    earlier = (at[:, None] > at[None, :]).astype(jnp.bfloat16)
    before = jnp.dot(earlier, hot, preferred_element_type=jnp.float32)
    code = jnp.sum(hot.astype(jnp.float32) * (before + (owner * CAP).astype(jnp.float32)[None, :]), axis=1)
    return jnp.concatenate([code.reshape(routes.shape[1], -1), gate_values.T], axis=0)


def placed_rows(codes, zh):
    code = codes[:2].astype(jnp.int32)
    slot, rank = code // CAP, code % CAP
    row = jnp.where(slot % 2 == zh, (slot // 2) * (2 * CAP) + rank, -2 * CAP)
    return jnp.stack([row, row + CAP], axis=1).reshape(2, -1)


def plane_rows():
    return 2 * CAP * lax.axis_size("y") * lax.axis_size("x")


def gather_rows(rows, table):
    at = jnp.arange(plane_rows(), dtype=jnp.int32)
    pick = ((rows[0][None, :] == at[:, None]) | (rows[1][None, :] == at[:, None])).astype(jnp.bfloat16)
    return jnp.dot(pick, table, preferred_element_type=jnp.float32).astype(jnp.bfloat16)


def exchange(rows, axes=PLANE):
    blocks = rows.reshape((lax.axis_size(axes), -1, rows.shape[-1]))
    return lax.all_to_all(blocks, axes, split_axis=0, concat_axis=0, tiled=True).reshape(rows.shape)


def expert_part(rows, weights):
    half = jnp.einsum("rd,gdf->grf", rows, weights[:2], preferred_element_type=jnp.float32)
    total = half + swap(half, "c")
    hidden = (jax.nn.silu(total[0]) * total[1]).astype(jnp.bfloat16)
    return lax.dot_general(
        hidden, weights[2], (((1,), (1,)), ((), ())), preferred_element_type=jnp.float32
    ).astype(jnp.bfloat16)


def weighted(back, codes, rows):
    at = jnp.arange(back.shape[0], dtype=jnp.int32)
    gate = jnp.concatenate([codes[2:4], codes[2:4]], axis=1)
    mix = sum(jnp.where(rows[k][:, None] == at[None, :], gate[k][:, None], 0.0) for k in range(2))
    high = mix.astype(jnp.bfloat16)
    low = (mix - high.astype(jnp.float32)).astype(jnp.bfloat16)
    return jnp.dot(high, back, preferred_element_type=jnp.float32) + jnp.dot(
        low, back, preferred_element_type=jnp.float32
    )


def by_columns(mixed, near):
    tok_rows = mixed.shape[0] // 2
    parts = mixed.astype(jnp.bfloat16).reshape(2, tok_rows, 2, near, -1)
    return jnp.transpose(parts, (3, 2, 1, 0, 4)).reshape(near, 2, tok_rows, -1)


def near_sum(parts, place, mine):
    count = parts.shape[0]
    total = lax.dynamic_index_in_dim(parts, place ^ mine, 0, keepdims=False).astype(jnp.float32)
    for step in range(1, count):
        block = lax.dynamic_index_in_dim(parts, place ^ step ^ mine, 0, keepdims=False)
        total += lax.ppermute(block, NEAR, [(i, i ^ step) for i in range(count)]).astype(jnp.float32)
    return total.astype(jnp.bfloat16)


tied = lax.optimization_barrier


def pick_pieces(spread, old_owner, new_owner, zh):
    moved = new_owner != old_owner
    low = jnp.min(jnp.where(moved, old_owner, old_owner.shape[0]))
    high = jnp.max(jnp.where(moved, old_owner, -1))
    low_piece = lax.dynamic_index_in_dim(spread, low >> 1, 0, keepdims=False)
    high_piece = lax.dynamic_index_in_dim(spread, high >> 1, 0, keepdims=False)
    low_here, high_here = (low & 1) == zh, (high & 1) == zh
    other = swap(jnp.where(low_here, low_piece, high_piece), "zh")
    to_low = jnp.where(high_here, high_piece, other)
    to_high = jnp.where(low_here, low_piece, other)
    slots = 2 * jnp.arange(spread.shape[0], dtype=jnp.int32)[:, None, None] + zh
    return jnp.where(slots == low, to_low[None], jnp.where(slots == high, to_high[None], spread))


def shards(tokens, routes, gate_values, expert_weights, old_owner, new_owner):
    zh, far, place = lax.axis_index("zh"), lax.axis_index("ma"), lax.axis_index(NEAR)
    near = lax.axis_size(NEAR)
    tok_rows = tokens.shape[0]
    own = expert_weights[0]
    table = jnp.transpose(tokens.reshape(tok_rows, 2 * near, 2, -1), (2, 0, 1, 3)).reshape(2 * tok_rows, -1)
    table = with_layout_constraint(table, Layout(major_to_minor=(0, 1)))
    share = 2 * tok_rows // near
    part = lax.dynamic_slice_in_dim(table, (near - 1 - place) * share, share, 0)
    codes = place_codes(routes, gate_values, old_owner)
    rows = placed_rows(codes, zh)
    quarter = mirrored(part)
    chips = lax.axis_size("y") * lax.axis_size("x")
    spread = lax.all_to_all(
        own.reshape(chips, -1, own.shape[-1]), ("y", "x"), split_axis=0, concat_axis=0, tiled=True
    )
    payload, spread, quarter, later_codes = tied((gather_rows(rows, table), spread, quarter, codes))
    sent = exchange(payload)
    other_codes = mirrored(later_codes)
    other_rows = placed_rows(other_codes, zh)
    other_table = lax.all_gather(quarter, NEAR, tiled=True)
    payload, sent = tied((gather_rows(other_rows, other_table), sent))
    other_sent = exchange(payload)
    payload, other_sent = tied((expert_part(sent, own), other_sent))
    back = exchange(payload)
    chosen = pick_pieces(spread, old_owner, new_owner, zh)
    payload, back, chosen = tied((expert_part(other_sent, own), back, chosen))
    other_back = exchange(payload)

    kept = near_sum(by_columns(weighted(back, codes, rows), near), place, 0)
    kept, other_back, chosen = tied((kept, other_back, chosen))
    arrived = lax.all_to_all(chosen, ("y", "x"), split_axis=0, concat_axis=0, tiled=True)
    other_kept = near_sum(by_columns(weighted(other_back, other_codes, other_rows), near), place, near - 1)

    def of(value, index):
        return lax.dynamic_index_in_dim(value, index, 0, keepdims=False)

    total = of(kept, far).astype(jnp.float32)
    total += swap(of(kept, 1 - far), "ma").astype(jnp.float32)
    total += mirrored(of(other_kept, 1 - far)).astype(jnp.float32)
    total += lax.ppermute(of(other_kept, far), RING, [(i, i ^ 11) for i in range(16)]).astype(jnp.float32)
    return total.astype(jnp.bfloat16), arrived.reshape(expert_weights.shape)


def solution(mesh):
    fine = Mesh(mesh.devices.reshape(4, 4, 2, 2, 2, 2, 2), ("y", "x", "zh", "c", "ma", "mb", "mc"))
    expert, mp = ("y", "x", "zh", "c"), ("ma", "mb", "mc")
    in_specs = (
        P(expert, None),
        P(expert, None),
        P(expert, None),
        P(expert, None, None, mp),
        P(),
        P(),
    )
    out_specs = (P(expert, mp), P(expert, None, None, mp))
    return jax.shard_map(shards, mesh=fine, in_specs=in_specs, out_specs=out_specs, check_vma=False)
```

```python
import jax
import jax.numpy as jnp
from jax import lax
from jax.experimental.layout import Layout, with_layout_constraint
from jax.sharding import Mesh, PartitionSpec as P

PLANE = ("y", "x", "c")
NEAR = ("mb", "mc")
RING = ("zh", "ma", "mb", "mc")
CAP = 16


def swap(value, axis):
    return lax.ppermute(value, axis, [(0, 1), (1, 0)])


def mirrored(value):
    return lax.ppermute(value, RING, [(i, 15 - i) for i in range(16)])


def place_codes(routes, gate_values, owner):
    experts = owner.shape[0]
    flat = routes.T.reshape(-1)
    count = flat.shape[0]
    ids = jnp.arange(experts, dtype=jnp.int32)
    hot = (flat[:, None] == ids[None, :]).astype(jnp.bfloat16)
    at = jnp.arange(count, dtype=jnp.int32)
    earlier = (at[:, None] > at[None, :]).astype(jnp.bfloat16)
    before = jnp.dot(earlier, hot, preferred_element_type=jnp.float32)
    code = jnp.sum(hot.astype(jnp.float32) * (before + (owner * CAP).astype(jnp.float32)[None, :]), axis=1)
    return jnp.concatenate([code.reshape(routes.shape[1], -1), gate_values.T], axis=0)


def placed_rows(codes, zh):
    code = codes[:2].astype(jnp.int32)
    slot, rank = code // CAP, code % CAP
    row = jnp.where(slot % 2 == zh, (slot // 2) * (2 * CAP) + rank, -2 * CAP)
    return jnp.stack([row, row + CAP], axis=1).reshape(2, -1)


def plane_rows():
    return 2 * CAP * lax.axis_size("y") * lax.axis_size("x")


def gather_rows(rows, table):
    at = jnp.arange(plane_rows(), dtype=jnp.int32)
    pick = ((rows[0][None, :] == at[:, None]) | (rows[1][None, :] == at[:, None])).astype(jnp.bfloat16)
    return jnp.dot(pick, table, preferred_element_type=jnp.float32).astype(jnp.bfloat16)


def exchange(rows, axes=PLANE):
    blocks = rows.reshape((lax.axis_size(axes), -1, rows.shape[-1]))
    return lax.all_to_all(blocks, axes, split_axis=0, concat_axis=0, tiled=True).reshape(rows.shape)


def expert_part(rows, weights):
    half = jnp.einsum("rd,gdf->grf", rows, weights[:2], preferred_element_type=jnp.float32)
    total = half + swap(half, "c")
    hidden = (jax.nn.silu(total[0]) * total[1]).astype(jnp.bfloat16)
    return lax.dot_general(
        hidden, weights[2], (((1,), (1,)), ((), ())), preferred_element_type=jnp.float32
    ).astype(jnp.bfloat16)


def weighted(back, codes, rows):
    at = jnp.arange(back.shape[0], dtype=jnp.int32)
    gate = jnp.concatenate([codes[2:4], codes[2:4]], axis=1)
    mix = sum(jnp.where(rows[k][:, None] == at[None, :], gate[k][:, None], 0.0) for k in range(2))
    high = mix.astype(jnp.bfloat16)
    low = (mix - high.astype(jnp.float32)).astype(jnp.bfloat16)
    return jnp.dot(high, back, preferred_element_type=jnp.float32) + jnp.dot(
        low, back, preferred_element_type=jnp.float32
    )


def by_columns(mixed, near):
    tok_rows = mixed.shape[0] // 2
    parts = mixed.astype(jnp.bfloat16).reshape(2, tok_rows, 2, near, -1)
    return jnp.transpose(parts, (3, 2, 1, 0, 4)).reshape(near, 2, tok_rows, -1)


def near_sum(parts, place, mine, beside):
    count = parts.shape[0]
    own = lax.dynamic_index_in_dim(parts, place ^ mine, 0, keepdims=False)
    own, beside = tied((own, beside))
    total = own.astype(jnp.float32)
    for step in range(1, count):
        block = lax.dynamic_index_in_dim(parts, place ^ step ^ mine, 0, keepdims=False)
        total += lax.ppermute(block, NEAR, [(i, i ^ step) for i in range(count)]).astype(jnp.float32)
    return total.astype(jnp.bfloat16), beside


tied = lax.optimization_barrier


def pick_pieces(spread, old_owner, new_owner, zh):
    moved = new_owner != old_owner
    low = jnp.min(jnp.where(moved, old_owner, old_owner.shape[0]))
    high = jnp.max(jnp.where(moved, old_owner, -1))
    low_piece = lax.dynamic_index_in_dim(spread, low >> 1, 0, keepdims=False)
    high_piece = lax.dynamic_index_in_dim(spread, high >> 1, 0, keepdims=False)
    low_here, high_here = (low & 1) == zh, (high & 1) == zh
    other = swap(jnp.where(low_here, low_piece, high_piece), "zh")
    to_low = jnp.where(high_here, high_piece, other)
    to_high = jnp.where(low_here, low_piece, other)
    slots = 2 * jnp.arange(spread.shape[0], dtype=jnp.int32)[:, None, None] + zh
    return jnp.where(slots == low, to_low[None], jnp.where(slots == high, to_high[None], spread))


def shards(tokens, routes, gate_values, expert_weights, old_owner, new_owner):
    zh, far, place = lax.axis_index("zh"), lax.axis_index("ma"), lax.axis_index(NEAR)
    near = lax.axis_size(NEAR)
    tok_rows = tokens.shape[0]
    own = expert_weights[0]
    table = jnp.transpose(tokens.reshape(tok_rows, 2 * near, 2, -1), (2, 0, 1, 3)).reshape(2 * tok_rows, -1)
    table = with_layout_constraint(table, Layout(major_to_minor=(0, 1)))
    share = 2 * tok_rows // near
    part = lax.dynamic_slice_in_dim(table, (near - 1 - place) * share, share, 0)
    codes = place_codes(routes, gate_values, old_owner)
    rows = placed_rows(codes, zh)
    quarter = mirrored(part)
    chips = lax.axis_size("y") * lax.axis_size("x")
    spread = lax.all_to_all(
        own.reshape(chips, -1, own.shape[-1]), ("y", "x"), split_axis=0, concat_axis=0, tiled=True
    )
    payload, spread, quarter, later_codes = tied((gather_rows(rows, table), spread, quarter, codes))
    sent = exchange(payload)
    other_codes = mirrored(later_codes)
    other_rows = placed_rows(other_codes, zh)
    other_table = lax.all_gather(quarter, NEAR, tiled=True)
    payload, sent = tied((gather_rows(other_rows, other_table), sent))
    other_sent = exchange(payload)
    chosen = pick_pieces(spread, old_owner, new_owner, zh)
    payload, other_sent, chosen = tied((expert_part(sent, own), other_sent, chosen))
    back = exchange(payload)
    payload, back = tied((expert_part(other_sent, own), back))
    other_back = exchange(payload)

    parts = by_columns(weighted(back, codes, rows), near)
    kept, other_back = near_sum(parts, place, 0, other_back)
    other_parts = by_columns(weighted(other_back, other_codes, other_rows), near)
    other_kept, chosen = near_sum(other_parts, place, near - 1, chosen)
    arrived = lax.all_to_all(chosen, ("y", "x"), split_axis=0, concat_axis=0, tiled=True)

    def of(value, index):
        return lax.dynamic_index_in_dim(value, index, 0, keepdims=False)

    total = of(kept, far).astype(jnp.float32)
    total += swap(of(kept, 1 - far), "ma").astype(jnp.float32)
    total += mirrored(of(other_kept, 1 - far)).astype(jnp.float32)
    total += lax.ppermute(of(other_kept, far), RING, [(i, i ^ 11) for i in range(16)]).astype(jnp.float32)
    return total.astype(jnp.bfloat16), arrived.reshape(expert_weights.shape)


def solution(mesh):
    fine = Mesh(mesh.devices.reshape(4, 4, 2, 2, 2, 2, 2), ("y", "x", "zh", "c", "ma", "mb", "mc"))
    expert, mp = ("y", "x", "zh", "c"), ("ma", "mb", "mc")
    in_specs = (
        P(expert, None),
        P(expert, None),
        P(expert, None),
        P(expert, None, None, mp),
        P(),
        P(),
    )
    out_specs = (P(expert, mp), P(expert, None, None, mp))
    return jax.shard_map(shards, mesh=fine, in_specs=in_specs, out_specs=out_specs, check_vma=False)
```

```python
import jax
import jax.numpy as jnp
from jax import lax
from jax.experimental.layout import Layout, with_layout_constraint
from jax.sharding import Mesh, PartitionSpec as P

PLANE = ("y", "x", "c")
NEAR = ("mb", "mc")
RING = ("zh", "ma", "mb", "mc")
CAP = 16


def swap(value, axis):
    return lax.ppermute(value, axis, [(0, 1), (1, 0)])


def mirrored(value):
    return lax.ppermute(value, RING, [(i, 15 - i) for i in range(16)])


def place_codes(routes, gate_values, owner):
    experts = owner.shape[0]
    flat = routes.T.reshape(-1)
    count = flat.shape[0]
    ids = jnp.arange(experts, dtype=jnp.int32)
    hot = (flat[:, None] == ids[None, :]).astype(jnp.bfloat16)
    at = jnp.arange(count, dtype=jnp.int32)
    earlier = (at[:, None] > at[None, :]).astype(jnp.bfloat16)
    before = jnp.dot(earlier, hot, preferred_element_type=jnp.float32)
    code = jnp.sum(hot.astype(jnp.float32) * (before + (owner * CAP).astype(jnp.float32)[None, :]), axis=1)
    return jnp.concatenate([code.reshape(routes.shape[1], -1), gate_values.T], axis=0)


def placed_rows(codes, zh):
    code = codes[:2].astype(jnp.int32)
    slot, rank = code // CAP, code % CAP
    row = jnp.where(slot % 2 == zh, (slot // 2) * (2 * CAP) + rank, -2 * CAP)
    return jnp.stack([row, row + CAP], axis=1).reshape(2, -1)


def plane_rows():
    return 2 * CAP * lax.axis_size("y") * lax.axis_size("x")


def gather_rows(rows, table):
    at = jnp.arange(plane_rows(), dtype=jnp.int32)
    pick = ((rows[0][None, :] == at[:, None]) | (rows[1][None, :] == at[:, None])).astype(jnp.bfloat16)
    return jnp.dot(pick, table, preferred_element_type=jnp.float32).astype(jnp.bfloat16)


def exchange(rows, axes=PLANE):
    blocks = rows.reshape((lax.axis_size(axes), -1, rows.shape[-1]))
    return lax.all_to_all(blocks, axes, split_axis=0, concat_axis=0, tiled=True).reshape(rows.shape)


def expert_part(rows, weights):
    half = jnp.einsum("rd,gdf->grf", rows, weights[:2], preferred_element_type=jnp.float32)
    total = half + swap(half, "c")
    hidden = (jax.nn.silu(total[0]) * total[1]).astype(jnp.bfloat16)
    return lax.dot_general(
        hidden, weights[2], (((1,), (1,)), ((), ())), preferred_element_type=jnp.float32
    ).astype(jnp.bfloat16)


def weighted(back, codes, rows):
    at = jnp.arange(back.shape[0], dtype=jnp.int32)
    gate = jnp.concatenate([codes[2:4], codes[2:4]], axis=1)
    mix = sum(jnp.where(rows[k][:, None] == at[None, :], gate[k][:, None], 0.0) for k in range(2))
    high = mix.astype(jnp.bfloat16)
    low = (mix - high.astype(jnp.float32)).astype(jnp.bfloat16)
    return jnp.dot(high, back, preferred_element_type=jnp.float32) + jnp.dot(
        low, back, preferred_element_type=jnp.float32
    )


def by_columns(mixed, near):
    tok_rows = mixed.shape[0] // 2
    parts = mixed.astype(jnp.bfloat16).reshape(2, tok_rows, 2, near, -1)
    return jnp.transpose(parts, (3, 2, 1, 0, 4)).reshape(near, 2, tok_rows, -1)


def near_sum(parts, place, mine, beside):
    count = parts.shape[0]
    own = lax.dynamic_index_in_dim(parts, place ^ mine, 0, keepdims=False)
    own, beside = tied((own, beside))
    total = own.astype(jnp.float32)
    for step in range(1, count):
        block = lax.dynamic_index_in_dim(parts, place ^ step ^ mine, 0, keepdims=False)
        total += lax.ppermute(block, NEAR, [(i, i ^ step) for i in range(count)]).astype(jnp.float32)
    return total.astype(jnp.bfloat16), beside


tied = lax.optimization_barrier


def pick_pieces(spread, old_owner, new_owner, zh):
    moved = new_owner != old_owner
    low = jnp.min(jnp.where(moved, old_owner, old_owner.shape[0]))
    high = jnp.max(jnp.where(moved, old_owner, -1))
    low_piece = lax.dynamic_index_in_dim(spread, low >> 1, 0, keepdims=False)
    high_piece = lax.dynamic_index_in_dim(spread, high >> 1, 0, keepdims=False)
    low_here, high_here = (low & 1) == zh, (high & 1) == zh
    other = swap(jnp.where(low_here, low_piece, high_piece), "zh")
    to_low = jnp.where(high_here, high_piece, other)
    to_high = jnp.where(low_here, low_piece, other)
    slots = 2 * jnp.arange(spread.shape[0], dtype=jnp.int32)[:, None, None] + zh
    return jnp.where(slots == low, to_low[None], jnp.where(slots == high, to_high[None], spread))


def shards(tokens, routes, gate_values, expert_weights, old_owner, new_owner):
    zh, far, place = lax.axis_index("zh"), lax.axis_index("ma"), lax.axis_index(NEAR)
    near = lax.axis_size(NEAR)
    tok_rows = tokens.shape[0]
    own = expert_weights[0]
    table = jnp.transpose(tokens.reshape(tok_rows, 2 * near, 2, -1), (2, 0, 1, 3)).reshape(2 * tok_rows, -1)
    table = with_layout_constraint(table, Layout(major_to_minor=(0, 1)))
    share = 2 * tok_rows // near
    part = lax.dynamic_slice_in_dim(table, (near - 1 - place) * share, share, 0)
    codes = place_codes(routes, gate_values, old_owner)
    rows = placed_rows(codes, zh)
    quarter = mirrored(part)
    chips = lax.axis_size("y") * lax.axis_size("x")
    spread = lax.all_to_all(
        own.reshape(chips, -1, own.shape[-1]), ("y", "x"), split_axis=0, concat_axis=0, tiled=True
    )
    other_codes = mirrored(codes)
    payload, spread, quarter, other_codes = tied((gather_rows(rows, table), spread, quarter, other_codes))
    sent = exchange(payload)
    other_rows = placed_rows(other_codes, zh)
    other_table = lax.all_gather(quarter, NEAR, tiled=True)
    payload, sent = tied((gather_rows(other_rows, other_table), sent))
    other_sent = exchange(payload)
    chosen = pick_pieces(spread, old_owner, new_owner, zh)
    payload, other_sent, chosen = tied((expert_part(sent, own), other_sent, chosen))
    back = exchange(payload)
    payload, back = tied((expert_part(other_sent, own), back))
    other_back = exchange(payload)

    parts = by_columns(weighted(back, codes, rows), near)
    kept, other_back = near_sum(parts, place, 0, other_back)
    other_parts = by_columns(weighted(other_back, other_codes, other_rows), near)
    other_kept, chosen = near_sum(other_parts, place, near - 1, chosen)
    arrived = lax.all_to_all(chosen, ("y", "x"), split_axis=0, concat_axis=0, tiled=True)

    def of(value, index):
        return lax.dynamic_index_in_dim(value, index, 0, keepdims=False)

    total = of(kept, far).astype(jnp.float32)
    total += swap(of(kept, 1 - far), "ma").astype(jnp.float32)
    total += mirrored(of(other_kept, 1 - far)).astype(jnp.float32)
    total += lax.ppermute(of(other_kept, far), RING, [(i, i ^ 11) for i in range(16)]).astype(jnp.float32)
    return total.astype(jnp.bfloat16), arrived.reshape(expert_weights.shape)


def solution(mesh):
    fine = Mesh(mesh.devices.reshape(4, 4, 2, 2, 2, 2, 2), ("y", "x", "zh", "c", "ma", "mb", "mc"))
    expert, mp = ("y", "x", "zh", "c"), ("ma", "mb", "mc")
    in_specs = (
        P(expert, None),
        P(expert, None),
        P(expert, None),
        P(expert, None, None, mp),
        P(),
        P(),
    )
    out_specs = (P(expert, mp), P(expert, None, None, mp))
    return jax.shard_map(shards, mesh=fine, in_specs=in_specs, out_specs=out_specs, check_vma=False)
```

```python
import jax
import jax.numpy as jnp
from jax import lax
from jax.experimental.layout import Layout, with_layout_constraint
from jax.sharding import Mesh, PartitionSpec as P

PLANE = ("y", "x", "c")
NEAR = ("mb", "mc")
RING = ("zh", "ma", "mb", "mc")
CAP = 16


def swap(value, axis):
    return lax.ppermute(value, axis, [(0, 1), (1, 0)])


def mirrored(value):
    return lax.ppermute(value, RING, [(i, 15 - i) for i in range(16)])


def place_codes(routes, gate_values, owner):
    experts = owner.shape[0]
    flat = routes.T.reshape(-1)
    count = flat.shape[0]
    ids = jnp.arange(experts, dtype=jnp.int32)
    hot = (flat[:, None] == ids[None, :]).astype(jnp.bfloat16)
    at = jnp.arange(count, dtype=jnp.int32)
    earlier = (at[:, None] > at[None, :]).astype(jnp.bfloat16)
    before = jnp.dot(earlier, hot, preferred_element_type=jnp.float32)
    code = jnp.sum(hot.astype(jnp.float32) * (before + (owner * CAP).astype(jnp.float32)[None, :]), axis=1)
    return jnp.concatenate([code.reshape(routes.shape[1], -1), gate_values.T], axis=0)


def placed_rows(codes, zh):
    code = codes[:2].astype(jnp.int32)
    slot, rank = code // CAP, code % CAP
    row = jnp.where(slot % 2 == zh, (slot // 2) * (2 * CAP) + rank, -2 * CAP)
    return jnp.stack([row, row + CAP], axis=1).reshape(2, -1)


def plane_rows():
    return 2 * CAP * lax.axis_size("y") * lax.axis_size("x")


def gather_rows(rows, table):
    at = jnp.arange(plane_rows(), dtype=jnp.int32)
    pick = ((rows[0][None, :] == at[:, None]) | (rows[1][None, :] == at[:, None])).astype(jnp.bfloat16)
    return jnp.dot(pick, table, preferred_element_type=jnp.float32).astype(jnp.bfloat16)


def exchange(rows, axes=PLANE):
    blocks = rows.reshape((lax.axis_size(axes), -1, rows.shape[-1]))
    return lax.all_to_all(blocks, axes, split_axis=0, concat_axis=0, tiled=True).reshape(rows.shape)


def expert_part(rows, weights):
    half = jnp.einsum("rd,gdf->grf", rows, weights[:2], preferred_element_type=jnp.float32)
    total = half + swap(half, "c")
    hidden = (jax.nn.silu(total[0]) * total[1]).astype(jnp.bfloat16)
    return lax.dot_general(
        hidden, weights[2], (((1,), (1,)), ((), ())), preferred_element_type=jnp.float32
    ).astype(jnp.bfloat16)


def weighted(back, codes, rows):
    at = jnp.arange(back.shape[0], dtype=jnp.int32)
    gate = jnp.concatenate([codes[2:4], codes[2:4]], axis=1)
    mix = sum(jnp.where(rows[k][:, None] == at[None, :], gate[k][:, None], 0.0) for k in range(2))
    high = mix.astype(jnp.bfloat16)
    low = (mix - high.astype(jnp.float32)).astype(jnp.bfloat16)
    return jnp.dot(high, back, preferred_element_type=jnp.float32) + jnp.dot(
        low, back, preferred_element_type=jnp.float32
    )


def by_columns(mixed, near):
    tok_rows = mixed.shape[0] // 2
    parts = mixed.astype(jnp.bfloat16).reshape(2, tok_rows, 2, near, -1)
    return jnp.transpose(parts, (3, 2, 1, 0, 4)).reshape(near, 2, tok_rows, -1)


def near_sum(parts, place, mine, beside):
    count = parts.shape[0]
    own = lax.dynamic_index_in_dim(parts, place ^ mine, 0, keepdims=False)
    own, beside = tied((own, beside))
    total = own.astype(jnp.float32)
    for step in range(1, count):
        block = lax.dynamic_index_in_dim(parts, place ^ step ^ mine, 0, keepdims=False)
        total += lax.ppermute(block, NEAR, [(i, i ^ step) for i in range(count)]).astype(jnp.float32)
    return total.astype(jnp.bfloat16), beside


tied = lax.optimization_barrier


def pick_pieces(spread, old_owner, new_owner, zh):
    moved = new_owner != old_owner
    low = jnp.min(jnp.where(moved, old_owner, old_owner.shape[0]))
    high = jnp.max(jnp.where(moved, old_owner, -1))
    low_piece = lax.dynamic_index_in_dim(spread, low >> 1, 0, keepdims=False)
    high_piece = lax.dynamic_index_in_dim(spread, high >> 1, 0, keepdims=False)
    low_here, high_here = (low & 1) == zh, (high & 1) == zh
    other = swap(jnp.where(low_here, low_piece, high_piece), "zh")
    to_low = jnp.where(high_here, high_piece, other)
    to_high = jnp.where(low_here, low_piece, other)
    slots = 2 * jnp.arange(spread.shape[0], dtype=jnp.int32)[:, None, None] + zh
    return jnp.where(slots == low, to_low[None], jnp.where(slots == high, to_high[None], spread))


def shards(tokens, routes, gate_values, expert_weights, old_owner, new_owner):
    zh, far, place = lax.axis_index("zh"), lax.axis_index("ma"), lax.axis_index(NEAR)
    near = lax.axis_size(NEAR)
    tok_rows = tokens.shape[0]
    own = expert_weights[0]
    table = jnp.transpose(tokens.reshape(tok_rows, 2 * near, 2, -1), (2, 0, 1, 3)).reshape(2 * tok_rows, -1)
    table = with_layout_constraint(table, Layout(major_to_minor=(0, 1)))
    share = 2 * tok_rows // near
    part = lax.dynamic_slice_in_dim(table, (near - 1 - place) * share, share, 0)
    codes = place_codes(routes, gate_values, old_owner)
    rows = placed_rows(codes, zh)
    quarter = mirrored(part)
    chips = lax.axis_size("y") * lax.axis_size("x")
    spread = lax.all_to_all(
        own.reshape(chips, -1, own.shape[-1]), ("y", "x"), split_axis=0, concat_axis=0, tiled=True
    )
    other_codes = mirrored(codes)
    payload, spread, quarter, other_codes = tied((gather_rows(rows, table), spread, quarter, other_codes))
    sent = exchange(payload)
    other_rows = placed_rows(other_codes, zh)
    other_table = lax.all_gather(quarter, NEAR, tiled=True)
    payload, sent = tied((gather_rows(other_rows, other_table), sent))
    other_sent = exchange(payload)
    chosen = pick_pieces(spread, old_owner, new_owner, zh)
    payload, other_sent, chosen = tied((expert_part(sent, own), other_sent, chosen))
    other_back = exchange(expert_part(other_sent, own))
    payload, other_back = tied((payload, other_back))
    back = exchange(payload)

    other_parts = by_columns(weighted(other_back, other_codes, other_rows), near)
    other_kept, back = near_sum(other_parts, place, near - 1, back)
    parts = by_columns(weighted(back, codes, rows), near)
    kept, chosen = near_sum(parts, place, 0, chosen)
    other_kept, chosen = tied((other_kept, chosen))
    arrived = lax.all_to_all(chosen, ("y", "x"), split_axis=0, concat_axis=0, tiled=True)

    def of(value, index):
        return lax.dynamic_index_in_dim(value, index, 0, keepdims=False)

    total = of(kept, far).astype(jnp.float32)
    total += swap(of(kept, 1 - far), "ma").astype(jnp.float32)
    total += mirrored(of(other_kept, 1 - far)).astype(jnp.float32)
    total += lax.ppermute(of(other_kept, far), RING, [(i, i ^ 11) for i in range(16)]).astype(jnp.float32)
    return total.astype(jnp.bfloat16), arrived.reshape(expert_weights.shape)


def solution(mesh):
    fine = Mesh(mesh.devices.reshape(4, 4, 2, 2, 2, 2, 2), ("y", "x", "zh", "c", "ma", "mb", "mc"))
    expert, mp = ("y", "x", "zh", "c"), ("ma", "mb", "mc")
    in_specs = (
        P(expert, None),
        P(expert, None),
        P(expert, None),
        P(expert, None, None, mp),
        P(),
        P(),
    )
    out_specs = (P(expert, mp), P(expert, None, None, mp))
    return jax.shard_map(shards, mesh=fine, in_specs=in_specs, out_specs=out_specs, check_vma=False)
```

```python
import jax
import jax.numpy as jnp
from jax import lax
from jax.experimental.layout import Layout, with_layout_constraint
from jax.sharding import Mesh, PartitionSpec as P

PLANE = ("y", "x", "c")
NEAR = ("mb", "mc")
RING = ("zh", "ma", "mb", "mc")
CAP = 16


def swap(value, axis):
    return lax.ppermute(value, axis, [(0, 1), (1, 0)])


def mirrored(value):
    return lax.ppermute(value, RING, [(i, 15 - i) for i in range(16)])


def place_codes(routes, gate_values, owner):
    experts = owner.shape[0]
    flat = routes.T.reshape(-1)
    count = flat.shape[0]
    ids = jnp.arange(experts, dtype=jnp.int32)
    hot = (flat[:, None] == ids[None, :]).astype(jnp.bfloat16)
    at = jnp.arange(count, dtype=jnp.int32)
    earlier = (at[:, None] > at[None, :]).astype(jnp.bfloat16)
    before = jnp.dot(earlier, hot, preferred_element_type=jnp.float32)
    code = jnp.sum(hot.astype(jnp.float32) * (before + (owner * CAP).astype(jnp.float32)[None, :]), axis=1)
    return jnp.concatenate([code.reshape(routes.shape[1], -1), gate_values.T], axis=0)


def placed_rows(codes, zh):
    code = codes[:2].astype(jnp.int32)
    slot, rank = code // CAP, code % CAP
    row = jnp.where(slot % 2 == zh, (slot // 2) * (2 * CAP) + rank, -2 * CAP)
    return jnp.stack([row, row + CAP], axis=1).reshape(2, -1)


def plane_rows():
    return 2 * CAP * lax.axis_size("y") * lax.axis_size("x")


def gather_rows(rows, table):
    at = jnp.arange(plane_rows(), dtype=jnp.int32)
    pick = ((rows[0][None, :] == at[:, None]) | (rows[1][None, :] == at[:, None])).astype(jnp.bfloat16)
    return jnp.dot(pick, table, preferred_element_type=jnp.float32).astype(jnp.bfloat16)


def exchange(rows, axes=PLANE):
    blocks = rows.reshape((lax.axis_size(axes), -1, rows.shape[-1]))
    return lax.all_to_all(blocks, axes, split_axis=0, concat_axis=0, tiled=True).reshape(rows.shape)


def expert_part(rows, weights):
    half = jnp.einsum("rd,gdf->grf", rows, weights[:2], preferred_element_type=jnp.float32)
    total = half + swap(half, "c")
    hidden = (jax.nn.silu(total[0]) * total[1]).astype(jnp.bfloat16)
    return lax.dot_general(
        hidden, weights[2], (((1,), (1,)), ((), ())), preferred_element_type=jnp.float32
    ).astype(jnp.bfloat16)


def weighted(back, codes, rows):
    at = jnp.arange(back.shape[0], dtype=jnp.int32)
    gate = jnp.concatenate([codes[2:4], codes[2:4]], axis=1)
    mix = sum(jnp.where(rows[k][:, None] == at[None, :], gate[k][:, None], 0.0) for k in range(2))
    high = mix.astype(jnp.bfloat16)
    low = (mix - high.astype(jnp.float32)).astype(jnp.bfloat16)
    return jnp.dot(high, back, preferred_element_type=jnp.float32) + jnp.dot(
        low, back, preferred_element_type=jnp.float32
    )


def by_columns(mixed, near):
    tok_rows = mixed.shape[0] // 2
    parts = mixed.astype(jnp.bfloat16).reshape(2, tok_rows, 2, near, -1)
    return jnp.transpose(parts, (3, 2, 1, 0, 4)).reshape(near, 2, tok_rows, -1)


def near_sum(parts, place, mine, beside):
    count = parts.shape[0]
    own = lax.dynamic_index_in_dim(parts, place ^ mine, 0, keepdims=False)
    own, beside = tied((own, beside))
    total = own.astype(jnp.float32)
    for step in range(1, count):
        block = lax.dynamic_index_in_dim(parts, place ^ step ^ mine, 0, keepdims=False)
        total += lax.ppermute(block, NEAR, [(i, i ^ step) for i in range(count)]).astype(jnp.float32)
    return total.astype(jnp.bfloat16), beside


tied = lax.optimization_barrier


def pick_pieces(spread, old_owner, new_owner, zh):
    moved = new_owner != old_owner
    low = jnp.min(jnp.where(moved, old_owner, old_owner.shape[0]))
    high = jnp.max(jnp.where(moved, old_owner, -1))
    low_piece = lax.dynamic_index_in_dim(spread, low >> 1, 0, keepdims=False)
    high_piece = lax.dynamic_index_in_dim(spread, high >> 1, 0, keepdims=False)
    low_here, high_here = (low & 1) == zh, (high & 1) == zh
    other = swap(jnp.where(low_here, low_piece, high_piece), "zh")
    to_low = jnp.where(high_here, high_piece, other)
    to_high = jnp.where(low_here, low_piece, other)
    slots = 2 * jnp.arange(spread.shape[0], dtype=jnp.int32)[:, None, None] + zh
    return jnp.where(slots == low, to_low[None], jnp.where(slots == high, to_high[None], spread))


def shards(tokens, routes, gate_values, expert_weights, old_owner, new_owner):
    zh, far, place = lax.axis_index("zh"), lax.axis_index("ma"), lax.axis_index(NEAR)
    near = lax.axis_size(NEAR)
    tok_rows = tokens.shape[0]
    own = expert_weights[0]
    table = jnp.transpose(tokens.reshape(tok_rows, 2 * near, 2, -1), (2, 0, 1, 3)).reshape(2 * tok_rows, -1)
    table = with_layout_constraint(table, Layout(major_to_minor=(0, 1)))
    share = 2 * tok_rows // near
    part = lax.dynamic_slice_in_dim(table, (near - 1 - place) * share, share, 0)
    codes = place_codes(routes, gate_values, old_owner)
    rows = placed_rows(codes, zh)
    quarter = mirrored(part)
    chips = lax.axis_size("y") * lax.axis_size("x")
    other_codes = mirrored(codes)
    sent = exchange(gather_rows(rows, table))
    pieces, sent, quarter, other_codes = tied((own.reshape(chips, -1, own.shape[-1]), sent, quarter, other_codes))
    spread = lax.all_to_all(pieces, ("y", "x"), split_axis=0, concat_axis=0, tiled=True)
    other_rows = placed_rows(other_codes, zh)
    other_table = lax.all_gather(quarter, NEAR, tiled=True)
    payload, spread = tied((gather_rows(other_rows, other_table), spread))
    other_sent = exchange(payload)
    chosen = pick_pieces(spread, old_owner, new_owner, zh)
    payload, other_sent, chosen = tied((expert_part(sent, own), other_sent, chosen))
    back = exchange(payload)
    payload, back = tied((expert_part(other_sent, own), back))
    other_back = exchange(payload)

    parts = by_columns(weighted(back, codes, rows), near)
    kept, other_back = near_sum(parts, place, 0, other_back)
    other_parts = by_columns(weighted(other_back, other_codes, other_rows), near)
    other_kept, chosen = near_sum(other_parts, place, near - 1, chosen)
    arrived = lax.all_to_all(chosen, ("y", "x"), split_axis=0, concat_axis=0, tiled=True)

    def of(value, index):
        return lax.dynamic_index_in_dim(value, index, 0, keepdims=False)

    total = of(kept, far).astype(jnp.float32)
    total += swap(of(kept, 1 - far), "ma").astype(jnp.float32)
    total += mirrored(of(other_kept, 1 - far)).astype(jnp.float32)
    total += lax.ppermute(of(other_kept, far), RING, [(i, i ^ 11) for i in range(16)]).astype(jnp.float32)
    return total.astype(jnp.bfloat16), arrived.reshape(expert_weights.shape)


def solution(mesh):
    fine = Mesh(mesh.devices.reshape(4, 4, 2, 2, 2, 2, 2), ("y", "x", "zh", "c", "ma", "mb", "mc"))
    expert, mp = ("y", "x", "zh", "c"), ("ma", "mb", "mc")
    in_specs = (
        P(expert, None),
        P(expert, None),
        P(expert, None),
        P(expert, None, None, mp),
        P(),
        P(),
    )
    out_specs = (P(expert, mp), P(expert, None, None, mp))
    return jax.shard_map(shards, mesh=fine, in_specs=in_specs, out_specs=out_specs, check_vma=False)
```

```python
import functools

import jax
import jax.numpy as jnp
from jax import lax
from jax.experimental import pallas as pl
from jax.experimental.pallas import tpu as pltpu
from jax.experimental.layout import Layout, with_layout_constraint
from jax.sharding import Mesh, PartitionSpec as P

PLANE = ("y", "x", "c")
NEAR = ("mb", "mc")
RING = ("zh", "ma", "mb", "mc")
CAP = 16


def swap(value, axis):
    return lax.ppermute(value, axis, [(0, 1), (1, 0)])


def mirrored(value):
    return lax.ppermute(value, RING, [(i, 15 - i) for i in range(16)])


def place_codes(routes, gate_values, owner):
    experts = owner.shape[0]
    flat = routes.T.reshape(-1)
    count = flat.shape[0]
    ids = jnp.arange(experts, dtype=jnp.int32)
    hot = (flat[:, None] == ids[None, :]).astype(jnp.bfloat16)
    at = jnp.arange(count, dtype=jnp.int32)
    earlier = (at[:, None] > at[None, :]).astype(jnp.bfloat16)
    before = jnp.dot(earlier, hot, preferred_element_type=jnp.float32)
    code = jnp.sum(hot.astype(jnp.float32) * (before + (owner * CAP).astype(jnp.float32)[None, :]), axis=1)
    return jnp.concatenate([code.reshape(routes.shape[1], -1), gate_values.T], axis=0)


def placed_rows(codes, zh):
    code = codes[:2].astype(jnp.int32)
    slot, rank = code // CAP, code % CAP
    row = jnp.where(slot % 2 == zh, (slot // 2) * (2 * CAP) + rank, -2 * CAP)
    return jnp.stack([row, row + CAP], axis=1).reshape(2, -1)


def plane_rows():
    return 2 * CAP * lax.axis_size("y") * lax.axis_size("x")


def gather_rows(rows, table):
    at = jnp.arange(plane_rows(), dtype=jnp.int32)
    pick = ((rows[0][None, :] == at[:, None]) | (rows[1][None, :] == at[:, None])).astype(jnp.bfloat16)
    return jnp.dot(pick, table, preferred_element_type=jnp.float32).astype(jnp.bfloat16)


def exchange(rows, axes=PLANE):
    blocks = rows.reshape((lax.axis_size(axes), -1, rows.shape[-1]))
    return lax.all_to_all(blocks, axes, split_axis=0, concat_axis=0, tiled=True).reshape(rows.shape)


def expert_part(rows, weights):
    half = jnp.einsum("rd,gdf->grf", rows, weights[:2], preferred_element_type=jnp.float32)
    total = half + swap(half, "c")
    hidden = (jax.nn.silu(total[0]) * total[1]).astype(jnp.bfloat16)
    return lax.dot_general(
        hidden, weights[2], (((1,), (1,)), ((), ())), preferred_element_type=jnp.float32
    ).astype(jnp.bfloat16)


def columns_kernel(near, high, low, back, out):
    total = jnp.dot(high[...], back[...], preferred_element_type=jnp.float32)
    total += jnp.dot(low[...], back[...], preferred_element_type=jnp.float32)
    total = total.astype(jnp.bfloat16)
    tok_rows = total.shape[0] // 2
    cols = total.shape[1] // (2 * near)
    for z in range(2 * near):
        base = z * cols // 128 * 128
        offset = z * cols - base
        span = -(-(offset + cols) // 128) * 128
        at = lax.broadcasted_iota(jnp.int32, (span, 2 * cols), 0) - offset
        to = lax.broadcasted_iota(jnp.int32, (span, 2 * cols), 1)
        block = jnp.zeros((2 * cols, tok_rows), jnp.float32)
        for half in range(2):
            hit = (at + half * cols == to) & (at >= 0) & (at < cols)
            take = jnp.where(hit, 1.0, 0.0).astype(jnp.bfloat16)
            rows = total[half * tok_rows : (half + 1) * tok_rows, base : base + span]
            block += lax.dot_general(take, rows, (((0,), (1,)), ((), ())), preferred_element_type=jnp.float32)
        out[z % near, z // near] = block.astype(jnp.bfloat16)


def combined(back, codes, rows, near):
    at = jnp.arange(back.shape[0], dtype=jnp.int32)
    gate = jnp.concatenate([codes[2:4], codes[2:4]], axis=1)
    mix = sum(jnp.where(rows[k][:, None] == at[None, :], gate[k][:, None], 0.0) for k in range(2))
    high = mix.astype(jnp.bfloat16)
    low = (mix - high.astype(jnp.float32)).astype(jnp.bfloat16)
    shape = (near, 2, back.shape[1] // near, mix.shape[0] // 2)
    flops = 4 * mix.shape[0] * back.shape[0] * back.shape[1]
    return pl.pallas_call(
        functools.partial(columns_kernel, near),
        out_shape=jax.ShapeDtypeStruct(shape, jnp.bfloat16),
        in_specs=[pl.BlockSpec(memory_space=pltpu.VMEM)] * 3,
        out_specs=pl.BlockSpec(memory_space=pltpu.VMEM),
        compiler_params=pltpu.CompilerParams(vmem_limit_bytes=32 * 2**20),
        cost_estimate=pl.CostEstimate(flops=flops, bytes_accessed=4 * back.size, transcendentals=0),
    )(high, low, back)


def near_sum(parts, place, mine, beside):
    count = parts.shape[0]
    own = lax.dynamic_index_in_dim(parts, place ^ mine, 0, keepdims=False)
    own, beside = tied((own, beside))
    total = own.astype(jnp.float32)
    for step in range(1, count):
        block = lax.dynamic_index_in_dim(parts, place ^ step ^ mine, 0, keepdims=False)
        total += lax.ppermute(block, NEAR, [(i, i ^ step) for i in range(count)]).astype(jnp.float32)
    return total.astype(jnp.bfloat16), beside


tied = lax.optimization_barrier


def pick_pieces(spread, old_owner, new_owner, zh):
    moved = new_owner != old_owner
    low = jnp.min(jnp.where(moved, old_owner, old_owner.shape[0]))
    high = jnp.max(jnp.where(moved, old_owner, -1))
    low_piece = lax.dynamic_index_in_dim(spread, low >> 1, 0, keepdims=False)
    high_piece = lax.dynamic_index_in_dim(spread, high >> 1, 0, keepdims=False)
    low_here, high_here = (low & 1) == zh, (high & 1) == zh
    other = swap(jnp.where(low_here, low_piece, high_piece), "zh")
    to_low = jnp.where(high_here, high_piece, other)
    to_high = jnp.where(low_here, low_piece, other)
    slots = 2 * jnp.arange(spread.shape[0], dtype=jnp.int32)[:, None, None] + zh
    return jnp.where(slots == low, to_low[None], jnp.where(slots == high, to_high[None], spread))


def shards(tokens, routes, gate_values, expert_weights, old_owner, new_owner):
    zh, far, place = lax.axis_index("zh"), lax.axis_index("ma"), lax.axis_index(NEAR)
    near = lax.axis_size(NEAR)
    tok_rows = tokens.shape[0]
    own = expert_weights[0]
    table = jnp.transpose(tokens.reshape(tok_rows, 2 * near, 2, -1), (2, 0, 1, 3)).reshape(2 * tok_rows, -1)
    table = with_layout_constraint(table, Layout(major_to_minor=(0, 1)))
    share = 2 * tok_rows // near
    part = lax.dynamic_slice_in_dim(table, (near - 1 - place) * share, share, 0)
    codes = place_codes(routes, gate_values, old_owner)
    rows = placed_rows(codes, zh)
    quarter = mirrored(part)
    chips = lax.axis_size("y") * lax.axis_size("x")
    spread = lax.all_to_all(
        own.reshape(chips, -1, own.shape[-1]), ("y", "x"), split_axis=0, concat_axis=0, tiled=True
    )
    other_codes = mirrored(codes)
    payload, spread, quarter, other_codes = tied((gather_rows(rows, table), spread, quarter, other_codes))
    sent = exchange(payload)
    other_rows = placed_rows(other_codes, zh)
    other_table = lax.all_gather(quarter, NEAR, tiled=True)
    payload, sent = tied((gather_rows(other_rows, other_table), sent))
    other_sent = exchange(payload)
    chosen = pick_pieces(spread, old_owner, new_owner, zh)
    payload, other_sent, chosen = tied((expert_part(sent, own), other_sent, chosen))
    back = exchange(payload)
    payload, back = tied((expert_part(other_sent, own), back))
    other_back = exchange(payload)

    parts = combined(back, codes, rows, near)
    kept, other_back = near_sum(parts, place, 0, other_back)
    other_parts = combined(other_back, other_codes, other_rows, near)
    other_kept, chosen = near_sum(other_parts, place, near - 1, chosen)
    arrived = lax.all_to_all(chosen, ("y", "x"), split_axis=0, concat_axis=0, tiled=True)

    def of(value, index):
        return lax.dynamic_index_in_dim(value, index, 0, keepdims=False)

    total = of(kept, far).astype(jnp.float32)
    total += swap(of(kept, 1 - far), "ma").astype(jnp.float32)
    total += mirrored(of(other_kept, 1 - far)).astype(jnp.float32)
    total += lax.ppermute(of(other_kept, far), RING, [(i, i ^ 11) for i in range(16)]).astype(jnp.float32)
    return total.astype(jnp.bfloat16).T, arrived.reshape(expert_weights.shape)


def solution(mesh):
    fine = Mesh(mesh.devices.reshape(4, 4, 2, 2, 2, 2, 2), ("y", "x", "zh", "c", "ma", "mb", "mc"))
    expert, mp = ("y", "x", "zh", "c"), ("ma", "mb", "mc")
    in_specs = (
        P(expert, None),
        P(expert, None),
        P(expert, None),
        P(expert, None, None, mp),
        P(),
        P(),
    )
    out_specs = (P(expert, mp), P(expert, None, None, mp))
    return jax.shard_map(shards, mesh=fine, in_specs=in_specs, out_specs=out_specs, check_vma=False)
```
